32 devices in a mesh: ray: 8 (over y, x, core), tile: 4 (over z).
Axes of the slice: x: 2, y: 2, z: 4, core: 2. Of those that a mesh axis runs over, the one named last changes fastest.
Arguments:
- data: float32 [65536], P(('ray', 'tile')), may hold values from -6 to 6
- blocks: bfloat16 [8, 4, 128, 128, 128], P('ray', 'tile'), may hold values from -0.1875 to 0.1875
- block_cols: int32 [8, 4, 128], P('ray', 'tile'), may hold values from 0 to 255, as said below
- block_rows: int32 [8, 4, 128], P('ray', 'tile'), may hold values from 0 to 63
- block_counts: int32 [8, 4], P('ray', 'tile'), may hold values from 1 to 128, as said below
- reg_weight: float32 [16, 64, 128], P('tile', 'ray'), may hold values from 0.05 to 0.5
Outputs:
- model: float32 [16, 64, 128], P('tile', 'ray')
- ray_vector: float32 [65536], P(('ray', 'tile'))
The draws below stay inside these ranges and needn't reach their ends.
Inputs may be any that keep to these rules, and one draw needn't show every extreme that they name: `block_counts`: some ray group has exactly 128 live blocks in some tile in every draw. `block_cols`: column c of a tile lies in the cells of ray index (c % 64) // 8. Of the 128 slots of one ray group in one tile, live or not, at most 32 name columns of one ray index, and in every draw 128 // 32 ray indices are named by exactly 32 slots.
All inputs are finite; a program needn't handle non-finite values.
Results may differ from the reference program's by a relative error of at most 0.0043.
Values may be sent and summed in bfloat16 or wider, within the bound.
A program may use at most 64 MiB of HBM per device.

```python
import math
import jax
import jax.numpy as jnp
from jax import lax

CZ = 128
RB = 128
CX = 4
CY = 8
NB = 128
ROWBLK = 64
ITERS = 2
NX = 16
NY = 64
RAYS = 65536
CAP = 32
N_RAY = 8
N_TILE = 4


def draw_block_counts(key, part):
    key = jax.random.fold_in(key, 7)
    first, second, third, fourth = jax.random.split(key, 4)
    level = jax.random.randint(first, (N_RAY, 1), 0, 4)
    jitter = jax.random.randint(second, (N_RAY, N_TILE), 0, NB // 16 + 1)
    counts = jnp.maximum(1, NB * 2 ** level // 8 - jitter)
    pick_ray = jax.random.randint(third, (), 0, N_RAY)
    pick_tile = jax.random.randint(fourth, (), 0, N_TILE)
    chosen = (jnp.arange(N_RAY)[:, None] == pick_ray) & (jnp.arange(N_TILE)[None, :] == pick_tile)
    return jnp.where(chosen, NB, counts).astype(jnp.int32)


def draw_block_cols(key, part):
    key = jax.random.fold_in(key, 11)
    first, second, third, fourth = jax.random.split(key, 4)
    many = N_RAY * N_TILE
    keys = jax.random.split(first, many)
    orders = jax.vmap(lambda one: jax.random.permutation(one, NB))(keys)
    offset = jax.random.randint(second, (many, 1), 0, N_RAY)
    owner = (orders // CAP + offset) % N_RAY
    across = jax.random.randint(third, (many, NB), 0, CX)
    within = jax.random.randint(fourth, (many, NB), 0, CY)
    columns = across * (CY * N_RAY) + owner * CY + within
    return columns.reshape(N_RAY, N_TILE, NB).astype(jnp.int32)


def plant(drawn, stream_key, smallest, top_value):
    longest = drawn.shape.index(max(drawn.shape))
    spots = []
    for shift in (0, 1):
        where = [jax.random.randint(jax.random.fold_in(stream_key, axis), (), 0, length) for axis, length in enumerate(drawn.shape)]
        where[longest] = (where[longest] + shift) % drawn.shape[longest]
        spots.append(tuple(where))
    return drawn.at[spots[0]].set(smallest).at[spots[1]].set(top_value)


def block_levels(own_key, shape, cuts, least, high):
    loudness = 1.0
    for dim, shards_of in cuts:
        steps = jax.random.uniform(jax.random.fold_in(jax.random.fold_in(own_key, 6), dim), (shards_of,), jnp.float32, least / len(cuts), high / len(cuts))
        loudness = loudness * jnp.repeat(jnp.exp(steps), shape[dim] // shards_of).reshape((-1,) + (1,) * (len(shape) - 1 - dim))
    return loudness


def gaussian(rng, extent, width, bound, cuts=(), kind=jnp.bfloat16):
    values = jax.random.normal(rng, extent, jnp.float32) * width
    if len(cuts) > 0:
        values = block_levels(rng, extent, cuts, -0.22, 0.18) * values
    return jnp.clip(values, min=-bound, max=bound).astype(kind)


def setup_inputs(seed: int = 0) -> dict:
    arg_keys = jax.random.split(jax.random.key(seed), 7)
    data = gaussian(arg_keys[0], (RAYS,), 1.0, 6.0, ((0, 32),), jnp.float32)
    blocks = gaussian(arg_keys[1], (N_RAY, N_TILE, NB, RB, CZ), 0.03125, 0.1875, ((0, 8), (1, 4)))
    block_cols = draw_block_cols(jax.random.fold_in(arg_keys[6], 71), 0)
    block_rows = plant(jax.random.randint(arg_keys[3], (N_RAY, N_TILE, NB), 0, ROWBLK), jax.random.fold_in(arg_keys[3], 1), 0, ROWBLK - 1).astype(jnp.int32)
    block_counts = draw_block_counts(jax.random.fold_in(arg_keys[6], 71), 0)
    reg_weight = jnp.clip(jnp.exp(math.log(0.5) - 2.3025851 * jax.random.uniform(arg_keys[5], (NX, NY, CZ), jnp.float32) ** block_levels(arg_keys[5], (NX, NY, CZ), ((0, 4), (1, 8)), -0.2, 0.2)), 0.05, 0.5)
    return dict(data=data, blocks=blocks, block_cols=block_cols, block_rows=block_rows, block_counts=block_counts, reg_weight=reg_weight)


eps = 1e-06

def laplace(field):
    padded = jnp.pad(field, 1)
    beside = padded[2:, 1:-1, 1:-1] + padded[:-2, 1:-1, 1:-1]
    beside = beside + padded[1:-1, 2:, 1:-1] + padded[1:-1, :-2, 1:-1]
    beside = beside + padded[1:-1, 1:-1, 2:] + padded[1:-1, 1:-1, :-2]
    return 6.0 * field - beside

def reference(data, blocks, block_cols, block_rows, block_counts, reg_weight):
    grid_y = CY * N_RAY
    tile_cols = CX * grid_y
    tiles = jnp.arange(N_TILE).astype(jnp.int32)[:, None]
    live = jnp.arange(NB).astype(jnp.int32)[None, None, :] < block_counts[:, :, None]
    flat_cols = (tiles[None, :, :] * tile_cols + block_cols).astype(jnp.int32)

    def forward(field):
        tiled = field.astype(jnp.bfloat16).reshape(N_TILE, tile_cols, CZ)

        def group(args):
            values, cols, rows, mask = args
            segment = tiled[tiles, cols].astype(jnp.float32)
            product = jnp.einsum('tbrc,tbc->tbr', values.astype(jnp.float32), segment)
            product = jnp.where(mask[:, :, None], product, 0.0)
            return jax.ops.segment_sum(product.reshape(-1, RB), rows.reshape(-1), num_segments=ROWBLK).reshape(-1)
        return lax.map(group, (blocks, block_cols, block_rows, live)).reshape(-1)

    def transpose(rays_half):
        grouped = rays_half.reshape(N_RAY, ROWBLK, RB)

        def add(total, args):
            values, rows, index, mask, vector = args
            picked = vector[rows].astype(jnp.float32)
            contrib = jnp.einsum('tbrc,tbr->tbc', values.astype(jnp.float32), picked)
            contrib = jnp.where(mask[:, :, None], contrib, 0.0)
            return (total + jax.ops.segment_sum(contrib.reshape(-1, CZ), index.reshape(-1), num_segments=N_TILE * tile_cols), None)
        total, _ = lax.scan(add, jnp.zeros((N_TILE * tile_cols, CZ), jnp.float32), (blocks, block_rows, flat_cols, live, grouped))
        return total.reshape(N_TILE * CX, grid_y, CZ)
    raw_rays = data
    raw_cells = jnp.zeros_like(reg_weight)
    v_prev = jnp.zeros_like(reg_weight)
    u_rays = data
    u_cells = raw_cells
    alpha_prev = jnp.float32(0.0)
    for section in range(ITERS + 1):
        if section > 0:
            raw_rays = forward(v_prev) - alpha_prev * u_rays
            raw_cells = reg_weight * laplace(v_prev) - alpha_prev * u_cells
        beta = jnp.sqrt(jnp.sum(raw_rays * raw_rays) + jnp.sum(raw_cells * raw_cells) + eps)
        z_field = transpose(raw_rays.astype(jnp.bfloat16)) + laplace(reg_weight * raw_cells)
        v_raw = z_field / beta - beta * v_prev
        alpha = jnp.sqrt(jnp.sum(v_raw * v_raw) + eps)
        u_rays = raw_rays / beta
        u_cells = raw_cells / beta
        v_now = v_raw / alpha
        if section == 0:
            w_dir = v_now
            phibar = beta
            rhobar = alpha
            model = jnp.zeros_like(reg_weight)
        else:
            rho = jnp.sqrt(rhobar * rhobar + beta * beta)
            cosine = rhobar / rho
            sine = beta / rho
            theta = sine * alpha
            rhobar = -cosine * alpha
            phi = cosine * phibar
            phibar = sine * phibar
            model = model + phi / rho * w_dir
            w_dir = v_now - theta / rho * w_dir
        v_prev = v_now
        alpha_prev = alpha
    return (model, u_rays)
```

```python
import functools

import jax
import jax.numpy as jnp
from jax import lax
from jax.experimental import pallas as pl
from jax.experimental.pallas import tpu as pltpu
from jax.sharding import PartitionSpec as P

MESH = pl.DeviceIdType.MESH
EPS = 1e-06
GROUP = 16
F32 = jnp.float32
BF16 = jnp.bfloat16


def total(x):
    return jnp.sum(jnp.sum(x, axis=0, keepdims=True), axis=1, keepdims=True)


def fold(x):
    acc = x[0:8] * x[0:8]
    for i in range(8, x.shape[0], 8):
        acc = acc + x[i : i + 8] * x[i : i + 8]
    return acc


def dot(a, b):
    return jnp.dot(a, b, preferred_element_type=F32)


def exact_dot(onehot, x):
    p1 = x.astype(BF16)
    rest = x - p1.astype(F32)
    p2 = rest.astype(BF16)
    p3 = (rest - p2.astype(F32)).astype(BF16)
    return dot(onehot, p1) + dot(onehot, p2) + dot(onehot, p3)


def laplace(cur, prev, nxt, xlo, xhi, size_y):
    rows, lanes = cur.shape
    iy = lax.broadcasted_iota(jnp.int32, cur.shape, 0) & (size_y - 1)
    iz = lax.broadcasted_iota(jnp.int32, cur.shape, 1)
    up = jnp.where(iy == 0, pltpu.roll(prev, rows - size_y + 1, 0), pltpu.roll(cur, 1, 0))
    down = jnp.where(
        iy == size_y - 1, pltpu.roll(nxt, size_y - 1, 0), pltpu.roll(cur, rows - 1, 0)
    )
    left = jnp.where(iz == 0, 0.0, pltpu.roll(cur, 1, 1))
    right = jnp.where(iz == lanes - 1, 0.0, pltpu.roll(cur, lanes - 1, 1))
    below = jnp.concatenate([xlo, cur[:-size_y]], axis=0)
    above = jnp.concatenate([cur[size_y:], xhi], axis=0)
    return 6.0 * cur - (above + below + down + up + right + left)


def kernel(
    n_ray,
    n_tile,
    size_x,
    size_y,
    data_ref,
    blocks_ref,
    cols_ref,
    rows_ref,
    count_ref,
    reg_ref,
    model_ref,
    out_ref,
    held,
    pick,
    prod,
    dfull,
    zbuf,
    zrecv,
    vfull,
    vhalo,
    yrecv,
    small,
    qbuf,
    qhalo_y,
    qhalo_x,
    last,
    ubuf,
    block_sem,
    a_send,
    a_recv,
    b_send,
    b_recv,
    d_send,
    d_recv,
    h_send,
    h_recv,
    e_send,
    e_recv,
    s_send,
    s_recv,
    q_send,
    q_recv,
    f_send,
    f_recv,
):
    me = lax.axis_index("ray")
    t = lax.axis_index("tile")
    slots, width, depth = held.shape
    cells = size_x * size_y
    tile_cols = n_ray * cells
    grid_y = n_ray * size_y
    share = data_ref.shape[0]
    row_blocks = share * n_tile
    groups = slots // GROUP

    def block_copy(g):
        part = pl.ds(g * GROUP, GROUP)
        return pltpu.make_async_copy(blocks_ref.at[part], held.at[part], block_sem.at[g])

    for g in range(groups):
        block_copy(g).start()

    def ray_peer(d):
        return lax.rem(me + d, n_ray)

    def tile_peer(d):
        return lax.rem(t + d, n_tile)

    bar = pltpu.get_barrier_semaphore()
    for d in range(1, n_ray):
        pl.semaphore_signal(bar, inc=1, device_id=(ray_peer(d), t), device_id_type=MESH)
    for d in range(1, n_tile):
        pl.semaphore_signal(bar, inc=1, device_id=(me, tile_peer(d)), device_id_type=MESH)
    pl.semaphore_wait(bar, n_ray + n_tile - 2)

    started = []

    def send(src, dst, send_sem, recv_sem, device):
        copy = pltpu.make_async_remote_copy(
            src_ref=src,
            dst_ref=dst,
            send_sem=send_sem,
            recv_sem=recv_sem,
            device_id=device,
            device_id_type=MESH,
        )
        copy.start()
        started.append(copy)
        return copy

    def to_tiles(ref, sends, recvs):
        return [
            send(ref, ref, sends.at[d - 1], recvs.at[d - 1], (me, tile_peer(d)))
            for d in range(1, n_tile)
        ]

    def to_rays(ref, sends, recvs):
        return [
            send(ref, ref, sends.at[d - 1], recvs.at[d - 1], (ray_peer(d), t))
            for d in range(1, n_ray)
        ]

    def arrived(copies):
        for copy in copies:
            copy.wait_recv()

    mine = pl.ds(pl.multiple_of(t * share, share), share)
    dfull[mine, :] = data_ref[...]
    copies = to_tiles(dfull.at[mine], a_send, a_recv)

    live = lax.broadcasted_iota(jnp.int32, (1, slots), 1) < count_ref[...]
    col = cols_ref[...]
    col_x = lax.shift_right_logical(col, grid_y.bit_length() - 1)
    col_y = col & (grid_y - 1)
    place = (
        lax.shift_right_logical(col_y, size_y.bit_length() - 1) * cells
        + col_x * size_y
        + (col_y & (size_y - 1))
    )
    place = jnp.where(live, place, -1)
    row = jnp.where(live, rows_ref[...], -1)
    to_col = jnp.where(
        lax.broadcasted_iota(jnp.int32, (tile_cols, slots), 0) == place, 1.0, 0.0
    ).astype(F32)
    to_row = jnp.where(
        lax.broadcasted_iota(jnp.int32, (row_blocks, slots), 0) == row, 1.0, 0.0
    ).astype(F32)
    from_col = to_col.T.astype(BF16)
    from_row = to_row.T.astype(BF16)
    to_col = to_col.astype(BF16)
    to_row = to_row.astype(BF16)
    reg = reg_ref[...]
    has_prev = jnp.where(me > 0, 1.0, 0.0).astype(F32)
    has_next = jnp.where(me < n_ray - 1, 1.0, 0.0).astype(F32)
    has_below = jnp.where(t > 0, 1.0, 0.0).astype(F32)
    has_above = jnp.where(t < n_tile - 1, 1.0, 0.0).astype(F32)

    def transposed(half, first):
        pick[0] = dot(from_row, half).astype(BF16)
        sub = lax.broadcasted_iota(jnp.int32, (GROUP, depth), 0)

        @pl.loop(0, groups)
        def _(g):
            if first:
                block_copy(g).wait()
            start = pl.multiple_of(g * GROUP, GROUP)
            lhs = pick[0, pl.ds(start, GROUP), :]
            acc = jnp.zeros((GROUP, depth), F32)
            for j in range(GROUP):
                acc = jnp.where(sub == j, dot(lhs, held[start + j]), acc)
            prod[pl.ds(start, GROUP), :] = acc

        return exact_dot(to_col, prod[...])

    def forward(field):
        hi = field.astype(BF16)
        lo = (field - hi.astype(F32)).astype(BF16)
        pick[0] = dot(from_col, hi).astype(BF16)
        pick[1] = dot(from_col, lo).astype(BF16)
        sub = lax.broadcasted_iota(jnp.int32, (2 * GROUP, width), 0) & (GROUP - 1)

        @pl.loop(0, groups)
        def _(g):
            start = pl.multiple_of(g * GROUP, GROUP)
            lhs = jnp.concatenate(
                [pick[0, pl.ds(start, GROUP), :], pick[1, pl.ds(start, GROUP), :]], axis=0
            )
            acc = jnp.zeros((2 * GROUP, width), F32)
            for j in range(GROUP):
                one = lax.dot_general(
                    lhs, held[start + j], (((1,), (1,)), ((), ())), preferred_element_type=F32
                )
                acc = jnp.where(sub == j, one, acc)
            prod[pl.ds(start, GROUP), :] = acc[:GROUP] + acc[GROUP:]

        return exact_dot(to_row, prod[...])

    def spread_z(s, z, squares):
        for p in range(n_ray):
            zbuf[s, p, 0:cells, :] = z[p * cells : (p + 1) * cells]
            zbuf[s, p, cells : cells + 8, :] = squares
        zrecv[s, me] = zbuf[s, me]
        return [
            send(
                zbuf.at[s, ray_peer(d)],
                zrecv.at[s, me],
                b_send.at[s, d - 1],
                b_recv.at[s, d - 1],
                (ray_peer(d), t),
            )
            for d in range(1, n_ray)
        ]

    def summed(ref, count):
        acc = ref[0]
        for i in range(1, count):
            acc = acc + ref[i]
        return acc

    own = pl.ds(pl.multiple_of(me * cells, cells), cells)
    before = pl.ds(pl.multiple_of(ray_peer(n_ray - 1) * cells, cells), cells)
    after = pl.ds(pl.multiple_of(ray_peer(1) * cells, cells), cells)

    def edges(ref, dst, sends, recvs):
        return [
            send(
                ref.at[pl.ds(cells - size_y, size_y)],
                dst.at[0],
                sends.at[0],
                recvs.at[0],
                (me, tile_peer(1)),
            ),
            send(
                ref.at[pl.ds(0, size_y)],
                dst.at[1],
                sends.at[1],
                recvs.at[1],
                (me, tile_peer(n_tile - 1)),
            ),
        ]

    arrived(copies)
    raw_rays = dfull[...]
    old_rays = None
    raw_cells = None
    v_prev = None
    for s in range(3):
        if s < 2:
            z = transposed(raw_rays.astype(BF16), s == 0)
            squares = fold(raw_rays)
            if s > 0:
                arrived(cell_copies)
                squares = squares + summed(small.at[1], n_tile)
            copies = spread_z(s, z, squares)
            if s > 0:
                arrived(q_copies)
                smooth = laplace(
                    qbuf[...],
                    qhalo_y[0] * has_prev,
                    qhalo_y[1] * has_next,
                    qhalo_x[0] * has_below,
                    qhalo_x[1] * has_above,
                    size_y,
                )
            arrived(copies)
            sums = summed(zrecv.at[s], n_ray)
            beta = jnp.sqrt(total(sums[cells:]) + EPS)
            if s == 0:
                v_raw = sums[:cells] / beta
            else:
                v_raw = (sums[:cells] + smooth) / beta - beta * v_prev
            field = vfull.at[s]
            field[own, :] = v_raw
            copies = to_rays(field.at[own], d_send.at[s], d_recv.at[s])
            halo_copies = edges(
                field.at[own], vhalo.at[s], h_send.at[s], h_recv.at[s]
            )
            arrived(copies)
            whole = field[...]
            small[2 * s, t] = fold(whole)
            alpha_copies = to_tiles(small.at[2 * s, t], s_send.at[2 * s], s_recv.at[2 * s])
            yrecv[s, t] = forward(whole)
            y_copies = to_tiles(yrecv.at[s, t], e_send.at[s], e_recv.at[s])
            arrived(halo_copies)
            smooth_v = reg * laplace(
                v_raw,
                field[before, :] * has_prev,
                field[after, :] * has_next,
                vhalo[s, 0] * has_below,
                vhalo[s, 1] * has_above,
                size_y,
            )
            arrived(alpha_copies)
            alpha = jnp.sqrt(total(summed(small.at[2 * s], n_tile)) + EPS)
            v_now = v_raw / alpha
            if s == 0:
                new_cells = smooth_v / alpha
            else:
                new_cells = smooth_v / alpha - alpha * (raw_cells / beta)
            small[2 * s + 1, t] = fold(new_cells)
            cell_copies = to_tiles(
                small.at[2 * s + 1, t], s_send.at[2 * s + 1], s_recv.at[2 * s + 1]
            )
            if s == 0:
                qbuf[...] = reg * new_cells
                q_copies = edges(qbuf, qhalo_x, q_send, q_recv) + [
                    send(
                        qbuf, qhalo_y.at[0], q_send.at[2], q_recv.at[2], (ray_peer(1), t)
                    ),
                    send(
                        qbuf,
                        qhalo_y.at[1],
                        q_send.at[3],
                        q_recv.at[3],
                        (ray_peer(n_ray - 1), t),
                    ),
                ]
            old_rays = raw_rays / beta
            if s == 0:
                w_dir = v_now
                phibar = beta
                rhobar = alpha
                model = None
            else:
                rho = jnp.sqrt(rhobar * rhobar + beta * beta)
                cosine = rhobar / rho
                sine = beta / rho
                theta = sine * alpha
                rhobar = -cosine * alpha
                phi = cosine * phibar
                phibar = sine * phibar
                model = phi / rho * w_dir
                w_dir = v_now - theta / rho * w_dir
            arrived(y_copies)
            raw_rays = summed(yrecv.at[s], n_tile) / alpha - alpha * old_rays
            raw_cells = new_cells
            v_prev = v_now
        else:
            arrived(cell_copies)
            last[me] = fold(raw_rays) + summed(small.at[3], n_tile)
            copies = to_rays(last.at[me], f_send, f_recv)
            arrived(copies)
            beta = jnp.sqrt(total(summed(last, n_ray)) + EPS)
            ubuf[...] = raw_rays
            out_ref[...] = ubuf[mine, :] / beta
            rho = jnp.sqrt(rhobar * rhobar + beta * beta)
            phi = rhobar / rho * phibar
            model_ref[...] = model + phi / rho * w_dir
    for copy in started:
        copy.wait_send()


def shards(n_ray, n_tile, data, blocks, block_cols, block_rows, block_counts, reg_weight):
    size_x, size_y, depth = reg_weight.shape
    slots, width = blocks.shape[2:4]
    cells = size_x * size_y
    share = data.shape[0] // width
    row_blocks = share * n_tile
    dma = pltpu.SemaphoreType.DMA
    pairs = [
        dma((n_tile - 1,)),
        dma((n_tile - 1,)),
        dma((2, n_ray - 1)),
        dma((2, n_ray - 1)),
        dma((2, n_ray - 1)),
        dma((2, n_ray - 1)),
        dma((2, 2)),
        dma((2, 2)),
        dma((2, n_tile - 1)),
        dma((2, n_tile - 1)),
        dma((4, n_tile - 1)),
        dma((4, n_tile - 1)),
        dma((4,)),
        dma((4,)),
        dma((n_ray - 1,)),
        dma((n_ray - 1,)),
    ]
    vmem = pl.BlockSpec(memory_space=pltpu.VMEM)
    model, rays = pl.pallas_call(
        functools.partial(kernel, n_ray, n_tile, size_x, size_y),
        out_shape=(
            jax.ShapeDtypeStruct((cells, depth), F32),
            jax.ShapeDtypeStruct((share, width), F32),
        ),
        in_specs=[vmem, pl.BlockSpec(memory_space=pl.ANY), vmem, vmem, vmem, vmem],
        out_specs=(vmem, vmem),
        scratch_shapes=[
            pltpu.VMEM((slots, width, depth), BF16),
            pltpu.VMEM((2, slots, depth), BF16),
            pltpu.VMEM((slots, depth), F32),
            pltpu.VMEM((row_blocks, width), F32),
            pltpu.VMEM((2, n_ray, cells + 8, depth), F32),
            pltpu.VMEM((2, n_ray, cells + 8, depth), F32),
            pltpu.VMEM((2, n_ray * cells, depth), F32),
            pltpu.VMEM((2, 2, size_y, depth), F32),
            pltpu.VMEM((2, n_tile, row_blocks, width), F32),
            pltpu.VMEM((4, n_tile, 8, depth), F32),
            pltpu.VMEM((cells, depth), F32),
            pltpu.VMEM((2, cells, depth), F32),
            pltpu.VMEM((2, size_y, depth), F32),
            pltpu.VMEM((n_ray, 8, depth), F32),
            pltpu.VMEM((row_blocks, width), F32),
            dma((slots // GROUP,)),
        ]
        + pairs,
        compiler_params=pltpu.CompilerParams(
            collective_id=0, has_side_effects=True, vmem_limit_bytes=48 * 2**20
        ),
    )(
        data.reshape(share, width),
        blocks.reshape(slots, width, depth),
        block_cols.reshape(1, slots),
        block_rows.reshape(1, slots),
        block_counts,
        reg_weight.reshape(cells, depth),
    )
    return model.reshape(size_x, size_y, depth), rays.reshape(-1)


def solution(mesh):
    return jax.shard_map(
        functools.partial(shards, mesh.shape["ray"], mesh.shape["tile"]),
        mesh=mesh,
        in_specs=(
            P(("ray", "tile")),
            P("ray", "tile", None, None, None),
            P("ray", "tile", None),
            P("ray", "tile", None),
            P("ray", "tile"),
            P("tile", "ray", None),
        ),
        out_specs=(P("tile", "ray", None), P(("ray", "tile"))),
        check_vma=False,
    )
```

```python
import functools

import jax
import jax.numpy as jnp
from jax import lax
from jax.experimental import pallas as pl
from jax.experimental.pallas import tpu as pltpu
from jax.sharding import PartitionSpec as P

MESH = pl.DeviceIdType.MESH
EPS = 1e-06
GROUP = 16
F32 = jnp.float32
BF16 = jnp.bfloat16


def total(x):
    return jnp.sum(jnp.sum(x, axis=0, keepdims=True), axis=1, keepdims=True)


def fold(x):
    acc = x[0:8] * x[0:8]
    for i in range(8, x.shape[0], 8):
        acc = acc + x[i : i + 8] * x[i : i + 8]
    return acc


def dot(a, b):
    return jnp.dot(a, b, preferred_element_type=F32)


def exact_dot(onehot, x):
    p1 = x.astype(BF16)
    rest = x - p1.astype(F32)
    p2 = rest.astype(BF16)
    p3 = (rest - p2.astype(F32)).astype(BF16)
    return dot(onehot, p1) + dot(onehot, p2) + dot(onehot, p3)


def laplace(cur, prev, nxt, xlo, xhi, size_y):
    rows, lanes = cur.shape
    iy = lax.broadcasted_iota(jnp.int32, cur.shape, 0) & (size_y - 1)
    iz = lax.broadcasted_iota(jnp.int32, cur.shape, 1)
    up = jnp.where(iy == 0, pltpu.roll(prev, rows - size_y + 1, 0), pltpu.roll(cur, 1, 0))
    down = jnp.where(
        iy == size_y - 1, pltpu.roll(nxt, size_y - 1, 0), pltpu.roll(cur, rows - 1, 0)
    )
    left = jnp.where(iz == 0, 0.0, pltpu.roll(cur, 1, 1))
    right = jnp.where(iz == lanes - 1, 0.0, pltpu.roll(cur, lanes - 1, 1))
    below = jnp.concatenate([xlo, cur[:-size_y]], axis=0)
    above = jnp.concatenate([cur[size_y:], xhi], axis=0)
    return 6.0 * cur - (above + below + down + up + right + left)


def kernel(
    n_ray,
    n_tile,
    size_x,
    size_y,
    data_hbm,
    blocks_ref,
    cols_hbm,
    rows_hbm,
    count_hbm,
    reg_hbm,
    model_ref,
    out_ref,
    cols_ref,
    rows_ref,
    count_ref,
    reg_ref,
    held,
    pick,
    prod,
    dfull,
    zbuf,
    zrecv,
    vfull,
    vhalo,
    yrecv,
    small,
    qbuf,
    qhalo_y,
    qhalo_x,
    last,
    ubuf,
    in_sem,
    block_sem,
    a_send,
    a_recv,
    b_send,
    b_recv,
    d_send,
    d_recv,
    h_send,
    h_recv,
    e_send,
    e_recv,
    s_send,
    s_recv,
    q_send,
    q_recv,
    f_send,
    f_recv,
):
    me = lax.axis_index("ray")
    t = lax.axis_index("tile")
    slots, width, depth = held.shape
    cells = size_x * size_y
    tile_cols = n_ray * cells
    grid_y = n_ray * size_y
    share = data_hbm.shape[0]
    row_blocks = share * n_tile
    groups = slots // GROUP

    def block_copy(g):
        part = pl.ds(g * GROUP, GROUP)
        return pltpu.make_async_copy(blocks_ref.at[part], held.at[part], block_sem.at[g])

    mine = pl.ds(pl.multiple_of(t * share, share), share)
    inputs = [
        pltpu.make_async_copy(src, dst, in_sem.at[i])
        for i, (src, dst) in enumerate(
            [
                (data_hbm, dfull.at[mine]),
                (cols_hbm, cols_ref),
                (rows_hbm, rows_ref),
                (count_hbm, count_ref),
                (reg_hbm, reg_ref),
            ]
        )
    ]
    for copy in inputs:
        copy.start()
    for g in range(groups):
        block_copy(g).start()

    def ray_peer(d):
        return lax.rem(me + d, n_ray)

    def tile_peer(d):
        return lax.rem(t + d, n_tile)

    bar = pltpu.get_barrier_semaphore()
    for d in range(1, n_ray):
        pl.semaphore_signal(bar, inc=1, device_id=(ray_peer(d), t), device_id_type=MESH)
    for d in range(1, n_tile):
        pl.semaphore_signal(bar, inc=1, device_id=(me, tile_peer(d)), device_id_type=MESH)
    pl.semaphore_wait(bar, n_ray + n_tile - 2)

    started = []

    def send(src, dst, send_sem, recv_sem, device):
        copy = pltpu.make_async_remote_copy(
            src_ref=src,
            dst_ref=dst,
            send_sem=send_sem,
            recv_sem=recv_sem,
            device_id=device,
            device_id_type=MESH,
        )
        copy.start()
        started.append(copy)
        return copy

    def to_tiles(ref, sends, recvs):
        return [
            send(ref, ref, sends.at[d - 1], recvs.at[d - 1], (me, tile_peer(d)))
            for d in range(1, n_tile)
        ]

    def to_rays(ref, sends, recvs):
        return [
            send(ref, ref, sends.at[d - 1], recvs.at[d - 1], (ray_peer(d), t))
            for d in range(1, n_ray)
        ]

    def arrived(copies):
        for copy in copies:
            copy.wait_recv()

    inputs[0].wait()
    copies = to_tiles(dfull.at[mine], a_send, a_recv)

    for copy in inputs[1:]:
        copy.wait()
    live = lax.broadcasted_iota(jnp.int32, (1, slots), 1) < count_ref[...]
    col = cols_ref[...]
    col_x = lax.shift_right_logical(col, grid_y.bit_length() - 1)
    col_y = col & (grid_y - 1)
    place = (
        lax.shift_right_logical(col_y, size_y.bit_length() - 1) * cells
        + col_x * size_y
        + (col_y & (size_y - 1))
    )
    place = jnp.where(live, place, -1)
    row = jnp.where(live, rows_ref[...], -1)
    to_col = jnp.where(
        lax.broadcasted_iota(jnp.int32, (tile_cols, slots), 0) == place, 1.0, 0.0
    ).astype(F32)
    to_row = jnp.where(
        lax.broadcasted_iota(jnp.int32, (row_blocks, slots), 0) == row, 1.0, 0.0
    ).astype(F32)
    from_col = to_col.T.astype(BF16)
    from_row = to_row.T.astype(BF16)
    to_col = to_col.astype(BF16)
    to_row = to_row.astype(BF16)
    reg = reg_ref[...]
    has_prev = jnp.where(me > 0, 1.0, 0.0).astype(F32)
    has_next = jnp.where(me < n_ray - 1, 1.0, 0.0).astype(F32)
    has_below = jnp.where(t > 0, 1.0, 0.0).astype(F32)
    has_above = jnp.where(t < n_tile - 1, 1.0, 0.0).astype(F32)

    def transposed(half, first):
        pick[...] = dot(from_row, half).astype(BF16)
        sub = lax.broadcasted_iota(jnp.int32, (GROUP, depth), 0)
        upper = (sub & 3) < 2
        even = (sub & 1) == 0
        quad = lax.shift_right_logical(sub, 2)

        @pl.loop(0, groups)
        def _(g):
            if first:
                block_copy(g).wait()
            start = pl.multiple_of(g * GROUP, GROUP)
            lhs = pick[pl.ds(start, GROUP), :].astype(F32)
            lhs = jnp.concatenate(
                [jnp.where(upper, lhs, 0.0), jnp.where(upper, 0.0, lhs)], axis=1
            ).astype(BF16)
            acc = jnp.zeros((GROUP, depth), F32)
            for q in range(GROUP // 4):
                four = [held[start + 4 * q + i] for i in range(4)]
                rhs = jnp.concatenate(
                    [
                        jnp.concatenate(four[:2], axis=1),
                        jnp.concatenate(four[2:], axis=1),
                    ],
                    axis=0,
                )
                both = dot(lhs, rhs)
                acc = jnp.where(quad == q, jnp.where(even, both[:, :depth], both[:, depth:]), acc)
            prod[pl.ds(start, GROUP), :] = acc

        return exact_dot(to_col, prod[...])

    def forward(field):
        hi = field.astype(BF16)
        lo = (field - hi.astype(F32)).astype(BF16)
        rhs = jnp.concatenate([dot(from_col, hi).T, dot(from_col, lo).T], axis=1).astype(BF16)
        lane = lax.broadcasted_iota(jnp.int32, (width, slots), 1)

        def step(g, acc):
            for j in range(GROUP):
                slot = g * GROUP + j
                both = dot(held[slot], rhs)
                acc = jnp.where(lane == slot, both[:, :slots] + both[:, slots:], acc)
            return acc

        acc = lax.fori_loop(0, groups, step, jnp.zeros((width, slots), F32))
        return exact_dot(to_row, acc.T)

    def spread_z(s, z, squares):
        for p in range(n_ray):
            zbuf[s, p, 0:cells, :] = z[p * cells : (p + 1) * cells]
            zbuf[s, p, cells : cells + 8, :] = squares
        zrecv[s, me] = zbuf[s, me]
        return [
            send(
                zbuf.at[s, ray_peer(d)],
                zrecv.at[s, me],
                b_send.at[s, d - 1],
                b_recv.at[s, d - 1],
                (ray_peer(d), t),
            )
            for d in range(1, n_ray)
        ]

    def summed(ref, count):
        acc = ref[0]
        for i in range(1, count):
            acc = acc + ref[i]
        return acc

    own = pl.ds(pl.multiple_of(me * cells, cells), cells)
    before = pl.ds(pl.multiple_of(ray_peer(n_ray - 1) * cells, cells), cells)
    after = pl.ds(pl.multiple_of(ray_peer(1) * cells, cells), cells)

    def edges(ref, dst, sends, recvs):
        return [
            send(
                ref.at[pl.ds(cells - size_y, size_y)],
                dst.at[0],
                sends.at[0],
                recvs.at[0],
                (me, tile_peer(1)),
            ),
            send(
                ref.at[pl.ds(0, size_y)],
                dst.at[1],
                sends.at[1],
                recvs.at[1],
                (me, tile_peer(n_tile - 1)),
            ),
        ]

    arrived(copies)
    raw_rays = dfull[...]
    old_rays = None
    raw_cells = None
    v_prev = None
    for s in range(3):
        if s < 2:
            z = transposed(raw_rays.astype(BF16), s == 0)
            squares = fold(raw_rays)
            if s > 0:
                arrived(cell_copies)
                squares = squares + summed(small.at[1], n_tile)
            copies = spread_z(s, z, squares)
            if s > 0:
                arrived(q_copies)
                smooth = laplace(
                    qbuf[...],
                    qhalo_y[0] * has_prev,
                    qhalo_y[1] * has_next,
                    qhalo_x[0] * has_below,
                    qhalo_x[1] * has_above,
                    size_y,
                )
            arrived(copies)
            sums = summed(zrecv.at[s], n_ray)
            beta = jnp.sqrt(total(sums[cells:]) + EPS)
            if s == 0:
                v_raw = sums[:cells] / beta
            else:
                v_raw = (sums[:cells] + smooth) / beta - beta * v_prev
            field = vfull.at[s]
            field[own, :] = v_raw
            copies = to_rays(field.at[own], d_send.at[s], d_recv.at[s])
            halo_copies = edges(
                field.at[own], vhalo.at[s], h_send.at[s], h_recv.at[s]
            )
            arrived(copies)
            whole = field[...]
            small[2 * s, t] = fold(whole)
            alpha_copies = to_tiles(small.at[2 * s, t], s_send.at[2 * s], s_recv.at[2 * s])
            yrecv[s, t] = forward(whole)
            y_copies = to_tiles(yrecv.at[s, t], e_send.at[s], e_recv.at[s])
            arrived(halo_copies)
            smooth_v = reg * laplace(
                v_raw,
                field[before, :] * has_prev,
                field[after, :] * has_next,
                vhalo[s, 0] * has_below,
                vhalo[s, 1] * has_above,
                size_y,
            )
            arrived(alpha_copies)
            alpha = jnp.sqrt(total(summed(small.at[2 * s], n_tile)) + EPS)
            v_now = v_raw / alpha
            if s == 0:
                new_cells = smooth_v / alpha
            else:
                new_cells = smooth_v / alpha - alpha * (raw_cells / beta)
            small[2 * s + 1, t] = fold(new_cells)
            cell_copies = to_tiles(
                small.at[2 * s + 1, t], s_send.at[2 * s + 1], s_recv.at[2 * s + 1]
            )
            if s == 0:
                qbuf[...] = reg * new_cells
                q_copies = edges(qbuf, qhalo_x, q_send, q_recv) + [
                    send(
                        qbuf, qhalo_y.at[0], q_send.at[2], q_recv.at[2], (ray_peer(1), t)
                    ),
                    send(
                        qbuf,
                        qhalo_y.at[1],
                        q_send.at[3],
                        q_recv.at[3],
                        (ray_peer(n_ray - 1), t),
                    ),
                ]
            old_rays = raw_rays / beta
            if s == 0:
                w_dir = v_now
                phibar = beta
                rhobar = alpha
                model = None
            else:
                rho = jnp.sqrt(rhobar * rhobar + beta * beta)
                cosine = rhobar / rho
                sine = beta / rho
                theta = sine * alpha
                rhobar = -cosine * alpha
                phi = cosine * phibar
                phibar = sine * phibar
                model = phi / rho * w_dir
                w_dir = v_now - theta / rho * w_dir
            arrived(y_copies)
            raw_rays = summed(yrecv.at[s], n_tile) / alpha - alpha * old_rays
            raw_cells = new_cells
            v_prev = v_now
        else:
            arrived(cell_copies)
            last[me] = fold(raw_rays) + summed(small.at[3], n_tile)
            copies = to_rays(last.at[me], f_send, f_recv)
            arrived(copies)
            beta = jnp.sqrt(total(summed(last, n_ray)) + EPS)
            ubuf[...] = raw_rays
            out_ref[...] = ubuf[mine, :] / beta
            rho = jnp.sqrt(rhobar * rhobar + beta * beta)
            phi = rhobar / rho * phibar
            model_ref[...] = model + phi / rho * w_dir
    for copy in started:
        copy.wait_send()


def shards(n_ray, n_tile, data, blocks, block_cols, block_rows, block_counts, reg_weight):
    size_x, size_y, depth = reg_weight.shape
    slots, width = blocks.shape[2:4]
    cells = size_x * size_y
    share = data.shape[0] // width
    row_blocks = share * n_tile
    dma = pltpu.SemaphoreType.DMA
    pairs = [
        dma((n_tile - 1,)),
        dma((n_tile - 1,)),
        dma((2, n_ray - 1)),
        dma((2, n_ray - 1)),
        dma((2, n_ray - 1)),
        dma((2, n_ray - 1)),
        dma((2, 2)),
        dma((2, 2)),
        dma((2, n_tile - 1)),
        dma((2, n_tile - 1)),
        dma((4, n_tile - 1)),
        dma((4, n_tile - 1)),
        dma((4,)),
        dma((4,)),
        dma((n_ray - 1,)),
        dma((n_ray - 1,)),
    ]
    vmem = pl.BlockSpec(memory_space=pltpu.VMEM)
    model, rays = pl.pallas_call(
        functools.partial(kernel, n_ray, n_tile, size_x, size_y),
        out_shape=(
            jax.ShapeDtypeStruct((cells, depth), F32),
            jax.ShapeDtypeStruct((share, width), F32),
        ),
        in_specs=[pl.BlockSpec(memory_space=pltpu.HBM)] * 6,
        out_specs=(vmem, vmem),
        scratch_shapes=[
            pltpu.VMEM((1, slots), jnp.int32),
            pltpu.VMEM((1, slots), jnp.int32),
            pltpu.VMEM((1, 1), jnp.int32),
            pltpu.VMEM((cells, depth), F32),
            pltpu.VMEM((slots, width, depth), BF16),
            pltpu.VMEM((slots, depth), BF16),
            pltpu.VMEM((slots, depth), F32),
            pltpu.VMEM((row_blocks, width), F32),
            pltpu.VMEM((2, n_ray, cells + 8, depth), F32),
            pltpu.VMEM((2, n_ray, cells + 8, depth), F32),
            pltpu.VMEM((2, n_ray * cells, depth), F32),
            pltpu.VMEM((2, 2, size_y, depth), F32),
            pltpu.VMEM((2, n_tile, row_blocks, width), F32),
            pltpu.VMEM((4, n_tile, 8, depth), F32),
            pltpu.VMEM((cells, depth), F32),
            pltpu.VMEM((2, cells, depth), F32),
            pltpu.VMEM((2, size_y, depth), F32),
            pltpu.VMEM((n_ray, 8, depth), F32),
            pltpu.VMEM((row_blocks, width), F32),
            dma((5,)),
            dma((slots // GROUP,)),
        ]
        + pairs,
        compiler_params=pltpu.CompilerParams(
            collective_id=0, has_side_effects=True, vmem_limit_bytes=64 * 2**20
        ),
    )(
        data.reshape(share, width),
        blocks.reshape(slots, width, depth),
        block_cols.reshape(1, slots),
        block_rows.reshape(1, slots),
        block_counts,
        reg_weight.reshape(cells, depth),
    )
    return model.reshape(size_x, size_y, depth), rays.reshape(-1)


def solution(mesh):
    return jax.shard_map(
        functools.partial(shards, mesh.shape["ray"], mesh.shape["tile"]),
        mesh=mesh,
        in_specs=(
            P(("ray", "tile")),
            P("ray", "tile", None, None, None),
            P("ray", "tile", None),
            P("ray", "tile", None),
            P("ray", "tile"),
            P("tile", "ray", None),
        ),
        out_specs=(P("tile", "ray", None), P(("ray", "tile"))),
        check_vma=False,
    )
```

```python
import functools

import jax
import jax.numpy as jnp
from jax import lax
from jax.experimental import pallas as pl
from jax.experimental.pallas import tpu as pltpu
from jax.sharding import PartitionSpec as P

MESH = pl.DeviceIdType.MESH
EPS = 1e-06
GROUP = 16
TILE = 16
F32 = jnp.float32
BF16 = jnp.bfloat16


def total(x):
    return jnp.sum(jnp.sum(x, axis=0, keepdims=True), axis=1, keepdims=True)


def fold(x):
    acc = x[0:8] * x[0:8]
    for i in range(8, x.shape[0], 8):
        acc = acc + x[i : i + 8] * x[i : i + 8]
    return acc


def dot(a, b):
    return jnp.dot(a, b, preferred_element_type=F32)


def exact_dot(onehot, x):
    p1 = x.astype(BF16)
    rest = x - p1.astype(F32)
    p2 = rest.astype(BF16)
    p3 = (rest - p2.astype(F32)).astype(BF16)
    return dot(onehot, p1) + dot(onehot, p2) + dot(onehot, p3)


def parts_of(row):
    p1 = row.astype(BF16).astype(F32)
    p2 = (row - p1).astype(BF16).astype(F32)
    p3 = row - p1 - p2
    at = lax.broadcasted_iota(jnp.int32, (TILE, row.shape[1]), 0)
    tile = jnp.where(at == 0, p1, jnp.where(at == 1, p2, jnp.where(at == 2, p3, 0.0)))
    return tile.astype(BF16)


def laplace(cur, prev, nxt, xlo, xhi, size_y):
    rows, lanes = cur.shape
    iy = lax.broadcasted_iota(jnp.int32, cur.shape, 0) & (size_y - 1)
    iz = lax.broadcasted_iota(jnp.int32, cur.shape, 1)
    up = jnp.where(iy == 0, pltpu.roll(prev, rows - size_y + 1, 0), pltpu.roll(cur, 1, 0))
    down = jnp.where(
        iy == size_y - 1, pltpu.roll(nxt, size_y - 1, 0), pltpu.roll(cur, rows - 1, 0)
    )
    left = jnp.where(iz == 0, 0.0, pltpu.roll(cur, 1, 1))
    right = jnp.where(iz == lanes - 1, 0.0, pltpu.roll(cur, lanes - 1, 1))
    below = jnp.concatenate([xlo, cur[:-size_y]], axis=0)
    above = jnp.concatenate([cur[size_y:], xhi], axis=0)
    return 6.0 * cur - (above + below + down + up + right + left)


def kernel(
    n_ray,
    n_tile,
    size_x,
    size_y,
    data_hbm,
    blocks_ref,
    cols_hbm,
    rows_hbm,
    count_hbm,
    reg_hbm,
    model_ref,
    out_ref,
    cols_ref,
    rows_ref,
    count_ref,
    reg_ref,
    held,
    pick,
    prod,
    dfull,
    zbuf,
    zrecv,
    vfull,
    vhalo,
    yrecv,
    small,
    qbuf,
    qhalo_y,
    qhalo_x,
    last,
    ubuf,
    in_sem,
    block_sem,
    a_send,
    a_recv,
    b_send,
    b_recv,
    d_send,
    d_recv,
    h_send,
    h_recv,
    e_send,
    e_recv,
    s_send,
    s_recv,
    q_send,
    q_recv,
    f_send,
    f_recv,
):
    me = lax.axis_index("ray")
    t = lax.axis_index("tile")
    slots, width, depth = held.shape
    cells = size_x * size_y
    tile_cols = n_ray * cells
    grid_y = n_ray * size_y
    share = data_hbm.shape[0]
    row_blocks = share * n_tile
    groups = slots // GROUP

    def block_copy(g):
        part = pl.ds(g * GROUP, GROUP)
        return pltpu.make_async_copy(blocks_ref.at[part], held.at[part], block_sem.at[g])

    mine = pl.ds(pl.multiple_of(t * share, share), share)
    inputs = [
        pltpu.make_async_copy(src, dst, in_sem.at[i])
        for i, (src, dst) in enumerate(
            [
                (data_hbm, dfull.at[mine]),
                (cols_hbm, cols_ref),
                (rows_hbm, rows_ref),
                (count_hbm, count_ref),
                (reg_hbm, reg_ref),
            ]
        )
    ]
    for copy in inputs:
        copy.start()
    for g in range(groups):
        block_copy(g).start()

    def ray_peer(d):
        return lax.rem(me + d, n_ray)

    def tile_peer(d):
        return lax.rem(t + d, n_tile)

    bar = pltpu.get_barrier_semaphore()
    for d in range(1, n_ray):
        pl.semaphore_signal(bar, inc=1, device_id=(ray_peer(d), t), device_id_type=MESH)
    for d in range(1, n_tile):
        pl.semaphore_signal(bar, inc=1, device_id=(me, tile_peer(d)), device_id_type=MESH)
    pl.semaphore_wait(bar, n_ray + n_tile - 2)

    started = []

    def send(src, dst, send_sem, recv_sem, device):
        copy = pltpu.make_async_remote_copy(
            src_ref=src,
            dst_ref=dst,
            send_sem=send_sem,
            recv_sem=recv_sem,
            device_id=device,
            device_id_type=MESH,
        )
        copy.start()
        started.append(copy)
        return copy

    def to_tiles(ref, sends, recvs):
        return [
            send(ref, ref, sends.at[d - 1], recvs.at[d - 1], (me, tile_peer(d)))
            for d in range(1, n_tile)
        ]

    def to_rays(ref, sends, recvs):
        return [
            send(ref, ref, sends.at[d - 1], recvs.at[d - 1], (ray_peer(d), t))
            for d in range(1, n_ray)
        ]

    def arrived(copies):
        for copy in copies:
            copy.wait_recv()

    inputs[0].wait()
    copies = to_tiles(dfull.at[mine], a_send, a_recv)

    for copy in inputs[1:]:
        copy.wait()
    live = lax.broadcasted_iota(jnp.int32, (1, slots), 1) < count_ref[...]
    col = cols_ref[...]
    col_x = lax.shift_right_logical(col, grid_y.bit_length() - 1)
    col_y = col & (grid_y - 1)
    place = (
        lax.shift_right_logical(col_y, size_y.bit_length() - 1) * cells
        + col_x * size_y
        + (col_y & (size_y - 1))
    )
    place = jnp.where(live, place, -1)
    row = jnp.where(live, rows_ref[...], -1)
    to_col = jnp.where(
        lax.broadcasted_iota(jnp.int32, (tile_cols, slots), 0) == place, 1.0, 0.0
    ).astype(F32)
    to_row = jnp.where(
        lax.broadcasted_iota(jnp.int32, (row_blocks, slots), 0) == row, 1.0, 0.0
    ).astype(F32)
    from_col = to_col.T.astype(BF16)
    from_row = to_row.T.astype(BF16)
    to_col = to_col.astype(BF16)
    to_row = to_row.astype(BF16)
    reg = reg_ref[...]
    has_prev = jnp.where(me > 0, 1.0, 0.0).astype(F32)
    has_next = jnp.where(me < n_ray - 1, 1.0, 0.0).astype(F32)
    has_below = jnp.where(t > 0, 1.0, 0.0).astype(F32)
    has_above = jnp.where(t < n_tile - 1, 1.0, 0.0).astype(F32)

    def transposed(half, first):
        pick[...] = dot(from_row, half).astype(BF16)
        sub = lax.broadcasted_iota(jnp.int32, (GROUP, depth), 0)
        upper = (sub & 3) < 2
        even = (sub & 1) == 0
        quad = lax.shift_right_logical(sub, 2)

        @pl.loop(0, groups)
        def _(g):
            if first:
                block_copy(g).wait()
            start = pl.multiple_of(g * GROUP, GROUP)
            lhs = pick[pl.ds(start, GROUP), :].astype(F32)
            lhs = jnp.concatenate(
                [jnp.where(upper, lhs, 0.0), jnp.where(upper, 0.0, lhs)], axis=1
            ).astype(BF16)
            acc = jnp.zeros((GROUP, depth), F32)
            for q in range(GROUP // 4):
                four = [held[start + 4 * q + i] for i in range(4)]
                rhs = jnp.concatenate(
                    [
                        jnp.concatenate(four[:2], axis=1),
                        jnp.concatenate(four[2:], axis=1),
                    ],
                    axis=0,
                )
                both = dot(lhs, rhs)
                acc = jnp.where(quad == q, jnp.where(even, both[:, :depth], both[:, depth:]), acc)
            prod[pl.ds(start, GROUP), :] = acc

        return exact_dot(to_col, prod[...])

    def forward(field):
        hi = field.astype(BF16)
        lo = (field - hi.astype(F32)).astype(BF16)
        rhs = jnp.concatenate([dot(from_col, hi).T, dot(from_col, lo).T], axis=1).astype(BF16)
        lane = lax.broadcasted_iota(jnp.int32, (width, slots), 1)

        def step(g, acc):
            for j in range(GROUP):
                slot = g * GROUP + j
                both = dot(held[slot], rhs)
                acc = jnp.where(lane == slot, both[:, :slots] + both[:, slots:], acc)
            return acc

        acc = lax.fori_loop(0, groups, step, jnp.zeros((width, slots), F32))
        return exact_dot(to_row, acc.T)

    def spread_z(s, z, squares):
        rows = parts_of(jnp.sum(squares, axis=0, keepdims=True))
        for p in range(n_ray):
            zbuf[s, p, 0:cells, :] = z[p * cells : (p + 1) * cells].astype(BF16)
            zbuf[s, p, cells : cells + TILE, :] = rows
        zrecv[s, me] = zbuf[s, me]
        return [
            send(
                zbuf.at[s, ray_peer(d)],
                zrecv.at[s, me],
                b_send.at[s, d - 1],
                b_recv.at[s, d - 1],
                (ray_peer(d), t),
            )
            for d in range(1, n_ray)
        ]

    def summed(ref, count):
        acc = ref[0].astype(F32)
        for i in range(1, count):
            acc = acc + ref[i].astype(F32)
        return acc

    own = pl.ds(pl.multiple_of(me * cells, cells), cells)
    before = pl.ds(pl.multiple_of(ray_peer(n_ray - 1) * cells, cells), cells)
    after = pl.ds(pl.multiple_of(ray_peer(1) * cells, cells), cells)

    def edges(ref, dst, sends, recvs):
        return [
            send(
                ref.at[pl.ds(cells - size_y, size_y)],
                dst.at[0],
                sends.at[0],
                recvs.at[0],
                (me, tile_peer(1)),
            ),
            send(
                ref.at[pl.ds(0, size_y)],
                dst.at[1],
                sends.at[1],
                recvs.at[1],
                (me, tile_peer(n_tile - 1)),
            ),
        ]

    arrived(copies)
    raw_rays = dfull[...]
    old_rays = None
    raw_cells = None
    v_prev = None
    for s in range(3):
        if s < 2:
            z = transposed(raw_rays.astype(BF16), s == 0)
            squares = fold(raw_rays)
            if s > 0:
                arrived(cell_copies)
                squares = squares + summed(small.at[1], n_tile)
            copies = spread_z(s, z, squares)
            if s > 0:
                arrived(q_copies)
                smooth = laplace(
                    qbuf[...],
                    qhalo_y[0] * has_prev,
                    qhalo_y[1] * has_next,
                    qhalo_x[0] * has_below,
                    qhalo_x[1] * has_above,
                    size_y,
                )
            arrived(copies)
            sums = summed(zrecv.at[s], n_ray)
            beta = jnp.sqrt(total(sums[cells:]) + EPS)
            if s == 0:
                v_raw = sums[:cells] / beta
            else:
                v_raw = (sums[:cells] + smooth) / beta - beta * v_prev
            field = vfull.at[s]
            field[own, :] = v_raw
            copies = to_rays(field.at[own], d_send.at[s], d_recv.at[s])
            halo_copies = edges(
                field.at[own], vhalo.at[s], h_send.at[s], h_recv.at[s]
            )
            arrived(copies)
            whole = field[...]
            small[2 * s, t] = fold(whole)
            alpha_copies = to_tiles(small.at[2 * s, t], s_send.at[2 * s], s_recv.at[2 * s])
            yrecv[s, t] = forward(whole).astype(BF16)
            y_copies = to_tiles(yrecv.at[s, t], e_send.at[s], e_recv.at[s])
            arrived(halo_copies)
            smooth_v = reg * laplace(
                v_raw,
                field[before, :] * has_prev,
                field[after, :] * has_next,
                vhalo[s, 0] * has_below,
                vhalo[s, 1] * has_above,
                size_y,
            )
            arrived(alpha_copies)
            alpha = jnp.sqrt(total(summed(small.at[2 * s], n_tile)) + EPS)
            v_now = v_raw / alpha
            if s == 0:
                new_cells = smooth_v / alpha
            else:
                new_cells = smooth_v / alpha - alpha * (raw_cells / beta)
            small[2 * s + 1, t] = fold(new_cells)
            cell_copies = to_tiles(
                small.at[2 * s + 1, t], s_send.at[2 * s + 1], s_recv.at[2 * s + 1]
            )
            if s == 0:
                qbuf[...] = reg * new_cells
                q_copies = edges(qbuf, qhalo_x, q_send, q_recv) + [
                    send(
                        qbuf, qhalo_y.at[0], q_send.at[2], q_recv.at[2], (ray_peer(1), t)
                    ),
                    send(
                        qbuf,
                        qhalo_y.at[1],
                        q_send.at[3],
                        q_recv.at[3],
                        (ray_peer(n_ray - 1), t),
                    ),
                ]
            old_rays = raw_rays / beta
            if s == 0:
                w_dir = v_now
                phibar = beta
                rhobar = alpha
                model = None
            else:
                rho = jnp.sqrt(rhobar * rhobar + beta * beta)
                cosine = rhobar / rho
                sine = beta / rho
                theta = sine * alpha
                rhobar = -cosine * alpha
                phi = cosine * phibar
                phibar = sine * phibar
                model = phi / rho * w_dir
                w_dir = v_now - theta / rho * w_dir
            arrived(y_copies)
            raw_rays = summed(yrecv.at[s], n_tile) / alpha - alpha * old_rays
            raw_cells = new_cells
            v_prev = v_now
        else:
            arrived(cell_copies)
            last[me] = fold(raw_rays) + summed(small.at[3], n_tile)
            earlier = list(started)
            copies = to_rays(last.at[me], f_send, f_recv)
            for copy in earlier:
                copy.wait_send()
            arrived(copies)
            beta = jnp.sqrt(total(summed(last, n_ray)) + EPS)
            ubuf[...] = raw_rays
            out_ref[...] = ubuf[mine, :] / beta
            rho = jnp.sqrt(rhobar * rhobar + beta * beta)
            phi = rhobar / rho * phibar
            model_ref[...] = model + phi / rho * w_dir
    for copy in copies:
        copy.wait_send()


def hand_out(model_in, rays_in, model_out, rays_out, sem):
    copies = [
        pltpu.make_async_copy(model_in, model_out, sem.at[0]),
        pltpu.make_async_copy(rays_in, rays_out, sem.at[1]),
    ]
    for copy in copies:
        copy.start()
    for copy in copies:
        copy.wait()


def shards(n_ray, n_tile, data, blocks, block_cols, block_rows, block_counts, reg_weight):
    size_x, size_y, depth = reg_weight.shape
    slots, width = blocks.shape[2:4]
    cells = size_x * size_y
    share = data.shape[0] // width
    row_blocks = share * n_tile
    dma = pltpu.SemaphoreType.DMA
    pairs = [
        dma((n_tile - 1,)),
        dma((n_tile - 1,)),
        dma((2, n_ray - 1)),
        dma((2, n_ray - 1)),
        dma((2, n_ray - 1)),
        dma((2, n_ray - 1)),
        dma((2, 2)),
        dma((2, 2)),
        dma((2, n_tile - 1)),
        dma((2, n_tile - 1)),
        dma((4, n_tile - 1)),
        dma((4, n_tile - 1)),
        dma((4,)),
        dma((4,)),
        dma((n_ray - 1,)),
        dma((n_ray - 1,)),
    ]
    vmem = pl.BlockSpec(memory_space=pltpu.VMEM)
    model, rays = pl.pallas_call(
        functools.partial(kernel, n_ray, n_tile, size_x, size_y),
        out_shape=(
            jax.ShapeDtypeStruct((cells, depth), F32),
            jax.ShapeDtypeStruct((share, width), F32),
        ),
        in_specs=[pl.BlockSpec(memory_space=pltpu.HBM)] * 6,
        out_specs=(vmem, vmem),
        scratch_shapes=[
            pltpu.VMEM((1, slots), jnp.int32),
            pltpu.VMEM((1, slots), jnp.int32),
            pltpu.VMEM((1, 1), jnp.int32),
            pltpu.VMEM((cells, depth), F32),
            pltpu.VMEM((slots, width, depth), BF16),
            pltpu.VMEM((slots, depth), BF16),
            pltpu.VMEM((slots, depth), F32),
            pltpu.VMEM((row_blocks, width), F32),
            pltpu.VMEM((2, n_ray, cells + TILE, depth), BF16),
            pltpu.VMEM((2, n_ray, cells + TILE, depth), BF16),
            pltpu.VMEM((2, n_ray * cells, depth), F32),
            pltpu.VMEM((2, 2, size_y, depth), F32),
            pltpu.VMEM((2, n_tile, row_blocks, width), BF16),
            pltpu.VMEM((4, n_tile, 8, depth), F32),
            pltpu.VMEM((cells, depth), F32),
            pltpu.VMEM((2, cells, depth), F32),
            pltpu.VMEM((2, size_y, depth), F32),
            pltpu.VMEM((n_ray, 8, depth), F32),
            pltpu.VMEM((row_blocks, width), F32),
            dma((5,)),
            dma((slots // GROUP,)),
        ]
        + pairs,
        compiler_params=pltpu.CompilerParams(
            collective_id=0, has_side_effects=True, vmem_limit_bytes=64 * 2**20
        ),
    )(
        data.reshape(share, width),
        blocks.reshape(slots, width, depth),
        block_cols.reshape(1, slots),
        block_rows.reshape(1, slots),
        block_counts,
        reg_weight.reshape(cells, depth),
    )
    hbm = pl.BlockSpec(memory_space=pltpu.HBM)
    model, rays = pl.pallas_call(
        hand_out,
        out_shape=(
            jax.ShapeDtypeStruct((cells, depth), F32),
            jax.ShapeDtypeStruct((share, width), F32),
        ),
        in_specs=[hbm, hbm],
        out_specs=(hbm, hbm),
        scratch_shapes=[dma((2,))],
        compiler_params=pltpu.CompilerParams(vmem_limit_bytes=64 * 2**20),
    )(model, rays)
    return model.reshape(size_x, size_y, depth), rays.reshape(-1)


def solution(mesh):
    return jax.shard_map(
        functools.partial(shards, mesh.shape["ray"], mesh.shape["tile"]),
        mesh=mesh,
        in_specs=(
            P(("ray", "tile")),
            P("ray", "tile", None, None, None),
            P("ray", "tile", None),
            P("ray", "tile", None),
            P("ray", "tile"),
            P("tile", "ray", None),
        ),
        out_specs=(P("tile", "ray", None), P(("ray", "tile"))),
        check_vma=False,
    )
```

```python
import functools

import jax
import jax.numpy as jnp
from jax import lax
from jax.experimental import pallas as pl
from jax.experimental.pallas import tpu as pltpu
from jax.sharding import PartitionSpec as P

MESH = pl.DeviceIdType.MESH
EPS = 1e-06
GROUP = 16
TILE = 16
SPAN = 4
CHUNK = 8
F32 = jnp.float32
BF16 = jnp.bfloat16


def total(x):
    return jnp.sum(jnp.sum(x, axis=0, keepdims=True), axis=1, keepdims=True)


def fold(x):
    acc = x[0:8] * x[0:8]
    for i in range(8, x.shape[0], 8):
        acc = acc + x[i : i + 8] * x[i : i + 8]
    return acc


def dot(a, b):
    return jnp.dot(a, b, preferred_element_type=F32)


def halves(x, axis):
    hi = x.astype(BF16)
    lo = (x - hi.astype(F32)).astype(BF16)
    return jnp.concatenate([hi, lo], axis=axis)


def parts_of(row):
    p1 = row.astype(BF16).astype(F32)
    p2 = (row - p1).astype(BF16).astype(F32)
    p3 = row - p1 - p2
    at = lax.broadcasted_iota(jnp.int32, (TILE, row.shape[1]), 0)
    tile = jnp.where(at == 0, p1, jnp.where(at == 1, p2, jnp.where(at == 2, p3, 0.0)))
    return tile.astype(BF16)


def laplace(cur, prev, nxt, xlo, xhi, size_y):
    rows, lanes = cur.shape
    iy = lax.broadcasted_iota(jnp.int32, cur.shape, 0) & (size_y - 1)
    iz = lax.broadcasted_iota(jnp.int32, cur.shape, 1)
    up = jnp.where(iy == 0, pltpu.roll(prev, rows - size_y + 1, 0), pltpu.roll(cur, 1, 0))
    down = jnp.where(
        iy == size_y - 1, pltpu.roll(nxt, size_y - 1, 0), pltpu.roll(cur, rows - 1, 0)
    )
    left = jnp.where(iz == 0, 0.0, pltpu.roll(cur, 1, 1))
    right = jnp.where(iz == lanes - 1, 0.0, pltpu.roll(cur, lanes - 1, 1))
    below = jnp.concatenate([xlo, cur[:-size_y]], axis=0)
    above = jnp.concatenate([cur[size_y:], xhi], axis=0)
    return 6.0 * cur - (above + below + down + up + right + left)


def kernel(
    n_ray,
    n_tile,
    size_x,
    size_y,
    data_hbm,
    blocks_ref,
    cols_hbm,
    rows_hbm,
    count_hbm,
    reg_hbm,
    model_ref,
    out_ref,
    cols_ref,
    rows_ref,
    count_ref,
    reg_ref,
    held,
    pick,
    prod,
    dfull,
    zbuf,
    zrecv,
    vfull,
    vhalo,
    yrecv,
    small,
    qbuf,
    qhalo_y,
    qhalo_x,
    last,
    ubuf,
    in_sem,
    block_sem,
    a_send,
    a_recv,
    b_send,
    b_recv,
    d_send,
    d_recv,
    h_send,
    h_recv,
    e_send,
    e_recv,
    s_send,
    s_recv,
    q_send,
    q_recv,
    f_send,
    f_recv,
):
    me = lax.axis_index("ray")
    t = lax.axis_index("tile")
    slots, width, depth = held.shape
    cells = size_x * size_y
    tile_cols = n_ray * cells
    grid_y = n_ray * size_y
    share = data_hbm.shape[0]
    row_blocks = share * n_tile
    groups = slots // GROUP

    def block_copy(g):
        part = pl.ds(g * GROUP, GROUP)
        return pltpu.make_async_copy(blocks_ref.at[part], held.at[part], block_sem.at[g])

    mine = pl.ds(pl.multiple_of(t * share, share), share)
    inputs = [
        pltpu.make_async_copy(src, dst, in_sem.at[i])
        for i, (src, dst) in enumerate(
            [
                (data_hbm, dfull.at[mine]),
                (cols_hbm, cols_ref),
                (rows_hbm, rows_ref),
                (count_hbm, count_ref),
                (reg_hbm, reg_ref),
            ]
        )
    ]
    for copy in inputs:
        copy.start()
    for g in range(groups):
        block_copy(g).start()

    def ray_peer(d):
        return lax.rem(me + d, n_ray)

    def tile_peer(d):
        return lax.rem(t + d, n_tile)

    bar = pltpu.get_barrier_semaphore()
    for d in range(1, n_ray):
        pl.semaphore_signal(bar, inc=1, device_id=(ray_peer(d), t), device_id_type=MESH)
    for d in range(1, n_tile):
        pl.semaphore_signal(bar, inc=1, device_id=(me, tile_peer(d)), device_id_type=MESH)
    pl.semaphore_wait(bar, n_ray + n_tile - 2)

    started = []

    def send(src, dst, send_sem, recv_sem, device):
        copy = pltpu.make_async_remote_copy(
            src_ref=src,
            dst_ref=dst,
            send_sem=send_sem,
            recv_sem=recv_sem,
            device_id=device,
            device_id_type=MESH,
        )
        copy.start()
        started.append(copy)
        return copy

    def to_tiles(ref, sends, recvs):
        return [
            send(ref, ref, sends.at[d - 1], recvs.at[d - 1], (me, tile_peer(d)))
            for d in range(1, n_tile)
        ]

    def to_rays(ref, sends, recvs):
        return [
            send(ref, ref, sends.at[d - 1], recvs.at[d - 1], (ray_peer(d), t))
            for d in range(1, n_ray)
        ]

    def arrived(copies):
        for copy in copies:
            copy.wait_recv()

    inputs[0].wait()
    copies = to_tiles(dfull.at[mine], a_send, a_recv)

    for copy in inputs[1:]:
        copy.wait()
    live = lax.broadcasted_iota(jnp.int32, (1, slots), 1) < count_ref[...]
    col = cols_ref[...]
    col_x = lax.shift_right_logical(col, grid_y.bit_length() - 1)
    col_y = col & (grid_y - 1)
    place = (
        lax.shift_right_logical(col_y, size_y.bit_length() - 1) * cells
        + col_x * size_y
        + (col_y & (size_y - 1))
    )
    place = jnp.where(live, place, -1)
    row = jnp.where(live, rows_ref[...], -1)
    to_col = jnp.where(
        lax.broadcasted_iota(jnp.int32, (tile_cols, slots), 0) == place, 1.0, 0.0
    ).astype(F32)
    to_row = jnp.where(
        lax.broadcasted_iota(jnp.int32, (row_blocks, slots), 0) == row, 1.0, 0.0
    ).astype(F32)
    from_col = to_col.T.astype(BF16)
    from_row = to_row.T.astype(BF16)
    to_col = jnp.concatenate([to_col, to_col], axis=1).astype(BF16)
    to_row = jnp.concatenate([to_row, to_row], axis=1).astype(BF16)
    reg = reg_ref[...]
    has_prev = jnp.where(me > 0, 1.0, 0.0).astype(F32)
    has_next = jnp.where(me < n_ray - 1, 1.0, 0.0).astype(F32)
    has_below = jnp.where(t > 0, 1.0, 0.0).astype(F32)
    has_above = jnp.where(t < n_tile - 1, 1.0, 0.0).astype(F32)

    def transposed(half, first):
        pick[...] = dot(from_row, half).astype(BF16)
        sub = lax.broadcasted_iota(jnp.int32, (GROUP, depth), 0)
        upper = (sub & 3) < 2
        even = (sub & 1) == 0
        quad = lax.shift_right_logical(sub, 2)

        @pl.loop(0, groups // SPAN)
        def _(i):
            for h in range(SPAN):
                g = i * SPAN + h
                if first:
                    block_copy(g).wait()
                start = pl.multiple_of(g * GROUP, GROUP)
                lhs = pick[pl.ds(start, GROUP), :].astype(F32)
                lhs = jnp.concatenate(
                    [jnp.where(upper, lhs, 0.0), jnp.where(upper, 0.0, lhs)], axis=1
                ).astype(BF16)
                acc = jnp.zeros((GROUP, depth), F32)
                for q in range(GROUP // 4):
                    four = [held[start + 4 * q + k] for k in range(4)]
                    rhs = jnp.concatenate(
                        [
                            jnp.concatenate(four[:2], axis=1),
                            jnp.concatenate(four[2:], axis=1),
                        ],
                        axis=0,
                    )
                    both = dot(lhs, rhs)
                    one = jnp.where(even, both[:, :depth], both[:, depth:])
                    acc = jnp.where(quad == q, one, acc)
                prod[pl.ds(start, GROUP), :] = acc

        return dot(to_col, halves(prod[...], 0))

    def forward(field):
        rhs = dot(from_col, halves(field, 1)).T.astype(BF16)
        lane = lax.broadcasted_iota(jnp.int32, (width, slots), 1)

        def step(g, acc):
            start = pl.multiple_of(g * CHUNK, CHUNK)
            lhs = held[pl.ds(start, CHUNK)].reshape(CHUNK * width, depth)
            out = dot(jnp.concatenate([lhs, lhs], axis=1), rhs)
            for j in range(CHUNK):
                acc = jnp.where(lane == start + j, out[j * width : (j + 1) * width], acc)
            return acc

        acc = lax.fori_loop(0, slots // CHUNK, step, jnp.zeros((width, slots), F32))
        return dot(to_row, halves(acc.T, 0))

    def spread_z(s, z, squares):
        rows = parts_of(jnp.sum(squares, axis=0, keepdims=True))
        for p in range(n_ray):
            zbuf[s, p, 0:cells, :] = z[p * cells : (p + 1) * cells].astype(BF16)
            zbuf[s, p, cells : cells + TILE, :] = rows
        zrecv[s, me] = zbuf[s, me]
        return [
            send(
                zbuf.at[s, ray_peer(d)],
                zrecv.at[s, me],
                b_send.at[s, d - 1],
                b_recv.at[s, d - 1],
                (ray_peer(d), t),
            )
            for d in range(1, n_ray)
        ]

    def summed(ref, count):
        acc = ref[0].astype(F32)
        for i in range(1, count):
            acc = acc + ref[i].astype(F32)
        return acc

    own = pl.ds(pl.multiple_of(me * cells, cells), cells)
    before = pl.ds(pl.multiple_of(ray_peer(n_ray - 1) * cells, cells), cells)
    after = pl.ds(pl.multiple_of(ray_peer(1) * cells, cells), cells)

    def edges(ref, dst, sends, recvs):
        return [
            send(
                ref.at[pl.ds(cells - size_y, size_y)],
                dst.at[0],
                sends.at[0],
                recvs.at[0],
                (me, tile_peer(1)),
            ),
            send(
                ref.at[pl.ds(0, size_y)],
                dst.at[1],
                sends.at[1],
                recvs.at[1],
                (me, tile_peer(n_tile - 1)),
            ),
        ]

    arrived(copies)
    raw_rays = dfull[...]
    old_rays = None
    raw_cells = None
    v_prev = None
    for s in range(3):
        if s < 2:
            z = transposed(raw_rays.astype(BF16), s == 0)
            squares = fold(raw_rays)
            if s > 0:
                arrived(cell_copies)
                squares = squares + summed(small.at[1], n_tile)
            copies = spread_z(s, z, squares)
            if s > 0:
                arrived(q_copies)
                smooth = laplace(
                    qbuf[...],
                    qhalo_y[0] * has_prev,
                    qhalo_y[1] * has_next,
                    qhalo_x[0] * has_below,
                    qhalo_x[1] * has_above,
                    size_y,
                )
            arrived(copies)
            sums = summed(zrecv.at[s], n_ray)
            beta = jnp.sqrt(total(sums[cells:]) + EPS)
            if s == 0:
                v_raw = sums[:cells] / beta
            else:
                v_raw = (sums[:cells] + smooth) / beta - beta * v_prev
            field = vfull.at[s]
            field[own, :] = v_raw
            copies = to_rays(field.at[own], d_send.at[s], d_recv.at[s])
            halo_copies = edges(
                field.at[own], vhalo.at[s], h_send.at[s], h_recv.at[s]
            )
            arrived(copies)
            whole = field[...]
            small[2 * s, t] = fold(whole)
            alpha_copies = to_tiles(small.at[2 * s, t], s_send.at[2 * s], s_recv.at[2 * s])
            yrecv[s, t] = forward(whole).astype(BF16)
            y_copies = to_tiles(yrecv.at[s, t], e_send.at[s], e_recv.at[s])
            arrived(halo_copies)
            smooth_v = reg * laplace(
                v_raw,
                field[before, :] * has_prev,
                field[after, :] * has_next,
                vhalo[s, 0] * has_below,
                vhalo[s, 1] * has_above,
                size_y,
            )
            arrived(alpha_copies)
            alpha = jnp.sqrt(total(summed(small.at[2 * s], n_tile)) + EPS)
            v_now = v_raw / alpha
            if s == 0:
                new_cells = smooth_v / alpha
            else:
                new_cells = smooth_v / alpha - alpha * (raw_cells / beta)
            small[2 * s + 1, t] = fold(new_cells)
            cell_copies = to_tiles(
                small.at[2 * s + 1, t], s_send.at[2 * s + 1], s_recv.at[2 * s + 1]
            )
            if s == 0:
                qbuf[...] = reg * new_cells
                q_copies = edges(qbuf, qhalo_x, q_send, q_recv) + [
                    send(
                        qbuf, qhalo_y.at[0], q_send.at[2], q_recv.at[2], (ray_peer(1), t)
                    ),
                    send(
                        qbuf,
                        qhalo_y.at[1],
                        q_send.at[3],
                        q_recv.at[3],
                        (ray_peer(n_ray - 1), t),
                    ),
                ]
            old_rays = raw_rays / beta
            if s == 0:
                w_dir = v_now
                phibar = beta
                rhobar = alpha
                model = None
            else:
                rho = jnp.sqrt(rhobar * rhobar + beta * beta)
                cosine = rhobar / rho
                sine = beta / rho
                theta = sine * alpha
                rhobar = -cosine * alpha
                phi = cosine * phibar
                phibar = sine * phibar
                model = phi / rho * w_dir
                w_dir = v_now - theta / rho * w_dir
            arrived(y_copies)
            raw_rays = summed(yrecv.at[s], n_tile) / alpha - alpha * old_rays
            raw_cells = new_cells
            v_prev = v_now
        else:
            arrived(cell_copies)
            last[me] = fold(raw_rays) + summed(small.at[3], n_tile)
            earlier = list(started)
            copies = to_rays(last.at[me], f_send, f_recv)
            for copy in earlier:
                copy.wait_send()
            arrived(copies)
            beta = jnp.sqrt(total(summed(last, n_ray)) + EPS)
            ubuf[...] = raw_rays
            out_ref[...] = ubuf[mine, :] / beta
            rho = jnp.sqrt(rhobar * rhobar + beta * beta)
            phi = rhobar / rho * phibar
            model_ref[...] = model + phi / rho * w_dir
    for copy in copies:
        copy.wait_send()


def hand_out(model_in, rays_in, model_out, rays_out, sem):
    copies = [
        pltpu.make_async_copy(model_in, model_out, sem.at[0]),
        pltpu.make_async_copy(rays_in, rays_out, sem.at[1]),
    ]
    for copy in copies:
        copy.start()
    for copy in copies:
        copy.wait()


def shards(n_ray, n_tile, data, blocks, block_cols, block_rows, block_counts, reg_weight):
    size_x, size_y, depth = reg_weight.shape
    slots, width = blocks.shape[2:4]
    cells = size_x * size_y
    share = data.shape[0] // width
    row_blocks = share * n_tile
    dma = pltpu.SemaphoreType.DMA
    pairs = [
        dma((n_tile - 1,)),
        dma((n_tile - 1,)),
        dma((2, n_ray - 1)),
        dma((2, n_ray - 1)),
        dma((2, n_ray - 1)),
        dma((2, n_ray - 1)),
        dma((2, 2)),
        dma((2, 2)),
        dma((2, n_tile - 1)),
        dma((2, n_tile - 1)),
        dma((4, n_tile - 1)),
        dma((4, n_tile - 1)),
        dma((4,)),
        dma((4,)),
        dma((n_ray - 1,)),
        dma((n_ray - 1,)),
    ]
    vmem = pl.BlockSpec(memory_space=pltpu.VMEM)
    model, rays = pl.pallas_call(
        functools.partial(kernel, n_ray, n_tile, size_x, size_y),
        out_shape=(
            jax.ShapeDtypeStruct((cells, depth), F32),
            jax.ShapeDtypeStruct((share, width), F32),
        ),
        in_specs=[pl.BlockSpec(memory_space=pltpu.HBM)] * 6,
        out_specs=(vmem, vmem),
        scratch_shapes=[
            pltpu.VMEM((1, slots), jnp.int32),
            pltpu.VMEM((1, slots), jnp.int32),
            pltpu.VMEM((1, 1), jnp.int32),
            pltpu.VMEM((cells, depth), F32),
            pltpu.VMEM((slots, width, depth), BF16),
            pltpu.VMEM((slots, depth), BF16),
            pltpu.VMEM((slots, depth), F32),
            pltpu.VMEM((row_blocks, width), F32),
            pltpu.VMEM((2, n_ray, cells + TILE, depth), BF16),
            pltpu.VMEM((2, n_ray, cells + TILE, depth), BF16),
            pltpu.VMEM((2, n_ray * cells, depth), F32),
            pltpu.VMEM((2, 2, size_y, depth), F32),
            pltpu.VMEM((2, n_tile, row_blocks, width), BF16),
            pltpu.VMEM((4, n_tile, 8, depth), F32),
            pltpu.VMEM((cells, depth), F32),
            pltpu.VMEM((2, cells, depth), F32),
            pltpu.VMEM((2, size_y, depth), F32),
            pltpu.VMEM((n_ray, 8, depth), F32),
            pltpu.VMEM((row_blocks, width), F32),
            dma((5,)),
            dma((slots // GROUP,)),
        ]
        + pairs,
        compiler_params=pltpu.CompilerParams(
            collective_id=0, has_side_effects=True, vmem_limit_bytes=64 * 2**20
        ),
    )(
        data.reshape(share, width),
        blocks.reshape(slots, width, depth),
        block_cols.reshape(1, slots),
        block_rows.reshape(1, slots),
        block_counts,
        reg_weight.reshape(cells, depth),
    )
    hbm = pl.BlockSpec(memory_space=pltpu.HBM)
    model, rays = pl.pallas_call(
        hand_out,
        out_shape=(
            jax.ShapeDtypeStruct((cells, depth), F32),
            jax.ShapeDtypeStruct((share, width), F32),
        ),
        in_specs=[hbm, hbm],
        out_specs=(hbm, hbm),
        scratch_shapes=[dma((2,))],
        compiler_params=pltpu.CompilerParams(vmem_limit_bytes=64 * 2**20),
    )(model, rays)
    return model.reshape(size_x, size_y, depth), rays.reshape(-1)


def solution(mesh):
    return jax.shard_map(
        functools.partial(shards, mesh.shape["ray"], mesh.shape["tile"]),
        mesh=mesh,
        in_specs=(
            P(("ray", "tile")),
            P("ray", "tile", None, None, None),
            P("ray", "tile", None),
            P("ray", "tile", None),
            P("ray", "tile"),
            P("tile", "ray", None),
        ),
        out_specs=(P("tile", "ray", None), P(("ray", "tile"))),
        check_vma=False,
    )
```

```python
import functools

import jax
import jax.numpy as jnp
from jax import lax
from jax.experimental import pallas as pl
from jax.experimental.pallas import tpu as pltpu
from jax.sharding import PartitionSpec as P

MESH = pl.DeviceIdType.MESH
EPS = 1e-06
GROUP = 16
TILE = 16
SPAN = 4
CHUNK = 4
F32 = jnp.float32
BF16 = jnp.bfloat16


def total(x):
    return jnp.sum(jnp.sum(x, axis=0, keepdims=True), axis=1, keepdims=True)


def fold(x):
    acc = x[0:8] * x[0:8]
    for i in range(8, x.shape[0], 8):
        acc = acc + x[i : i + 8] * x[i : i + 8]
    return acc


def dot(a, b):
    return jnp.dot(a, b, preferred_element_type=F32)


def halves(x, axis):
    hi = x.astype(BF16)
    lo = (x - hi.astype(F32)).astype(BF16)
    return jnp.concatenate([hi, lo], axis=axis)


def parts_of(row):
    p1 = row.astype(BF16).astype(F32)
    p2 = (row - p1).astype(BF16).astype(F32)
    p3 = row - p1 - p2
    at = lax.broadcasted_iota(jnp.int32, (TILE, row.shape[1]), 0)
    tile = jnp.where(at == 0, p1, jnp.where(at == 1, p2, jnp.where(at == 2, p3, 0.0)))
    return tile.astype(BF16)


def laplace(cur, prev, nxt, xlo, xhi, size_y):
    rows, lanes = cur.shape
    iy = lax.broadcasted_iota(jnp.int32, cur.shape, 0) & (size_y - 1)
    iz = lax.broadcasted_iota(jnp.int32, cur.shape, 1)
    up = jnp.where(iy == 0, pltpu.roll(prev, rows - size_y + 1, 0), pltpu.roll(cur, 1, 0))
    down = jnp.where(
        iy == size_y - 1, pltpu.roll(nxt, size_y - 1, 0), pltpu.roll(cur, rows - 1, 0)
    )
    left = jnp.where(iz == 0, 0.0, pltpu.roll(cur, 1, 1))
    right = jnp.where(iz == lanes - 1, 0.0, pltpu.roll(cur, lanes - 1, 1))
    below = jnp.concatenate([xlo, cur[:-size_y]], axis=0)
    above = jnp.concatenate([cur[size_y:], xhi], axis=0)
    return 6.0 * cur - (above + below + down + up + right + left)


def kernel(
    n_ray,
    n_tile,
    size_x,
    size_y,
    data_hbm,
    blocks_ref,
    cols_hbm,
    rows_hbm,
    count_hbm,
    reg_hbm,
    model_ref,
    out_ref,
    cols_ref,
    rows_ref,
    count_ref,
    reg_ref,
    held,
    pick,
    prod,
    dfull,
    zbuf,
    zrecv,
    vfull,
    vhalo,
    yrecv,
    small,
    qbuf,
    qhalo_y,
    qhalo_x,
    last,
    ubuf,
    in_sem,
    block_sem,
    a_send,
    a_recv,
    b_send,
    b_recv,
    d_send,
    d_recv,
    h_send,
    h_recv,
    e_send,
    e_recv,
    s_send,
    s_recv,
    q_send,
    q_recv,
    f_send,
    f_recv,
):
    me = lax.axis_index("ray")
    t = lax.axis_index("tile")
    slots, width, depth = held.shape
    cells = size_x * size_y
    tile_cols = n_ray * cells
    grid_y = n_ray * size_y
    share = data_hbm.shape[0]
    row_blocks = share * n_tile
    groups = slots // GROUP

    def block_copy(g):
        part = pl.ds(g * GROUP, GROUP)
        return pltpu.make_async_copy(blocks_ref.at[part], held.at[part], block_sem.at[g])

    mine = pl.ds(pl.multiple_of(t * share, share), share)
    inputs = [
        pltpu.make_async_copy(src, dst, in_sem.at[i])
        for i, (src, dst) in enumerate(
            [
                (data_hbm, dfull.at[mine]),
                (cols_hbm, cols_ref),
                (rows_hbm, rows_ref),
                (count_hbm, count_ref),
                (reg_hbm, reg_ref),
            ]
        )
    ]
    for copy in inputs:
        copy.start()
    for g in range(groups):
        block_copy(g).start()

    def ray_peer(d):
        return lax.rem(me + d, n_ray)

    def tile_peer(d):
        return lax.rem(t + d, n_tile)

    bar = pltpu.get_barrier_semaphore()
    for d in range(1, n_ray):
        pl.semaphore_signal(bar, inc=1, device_id=(ray_peer(d), t), device_id_type=MESH)
    for d in range(1, n_tile):
        pl.semaphore_signal(bar, inc=1, device_id=(me, tile_peer(d)), device_id_type=MESH)
    pl.semaphore_wait(bar, n_ray + n_tile - 2)

    started = []

    def send(src, dst, send_sem, recv_sem, device):
        copy = pltpu.make_async_remote_copy(
            src_ref=src,
            dst_ref=dst,
            send_sem=send_sem,
            recv_sem=recv_sem,
            device_id=device,
            device_id_type=MESH,
        )
        copy.start()
        started.append(copy)
        return copy

    def to_tiles(ref, sends, recvs):
        return [
            send(ref, ref, sends.at[d - 1], recvs.at[d - 1], (me, tile_peer(d)))
            for d in range(1, n_tile)
        ]

    def to_rays(ref, sends, recvs):
        return [
            send(ref, ref, sends.at[d - 1], recvs.at[d - 1], (ray_peer(d), t))
            for d in range(1, n_ray)
        ]

    def arrived(copies):
        for copy in copies:
            copy.wait_recv()

    inputs[0].wait()
    copies = to_tiles(dfull.at[mine], a_send, a_recv)

    for copy in inputs[1:]:
        copy.wait()
    live = lax.broadcasted_iota(jnp.int32, (1, slots), 1) < count_ref[...]
    col = cols_ref[...]
    col_x = lax.shift_right_logical(col, grid_y.bit_length() - 1)
    col_y = col & (grid_y - 1)
    place = (
        lax.shift_right_logical(col_y, size_y.bit_length() - 1) * cells
        + col_x * size_y
        + (col_y & (size_y - 1))
    )
    place = jnp.where(live, place, -1)
    row = jnp.where(live, rows_ref[...], -1)
    to_col = jnp.where(
        lax.broadcasted_iota(jnp.int32, (tile_cols, slots), 0) == place, 1.0, 0.0
    ).astype(F32)
    to_row = jnp.where(
        lax.broadcasted_iota(jnp.int32, (row_blocks, slots), 0) == row, 1.0, 0.0
    ).astype(F32)
    from_col = to_col.T.astype(BF16)
    from_row = to_row.T.astype(BF16)
    to_col = jnp.concatenate([to_col, to_col], axis=1).astype(BF16)
    to_row = jnp.concatenate([to_row, to_row], axis=1).astype(BF16)
    reg = reg_ref[...]
    has_prev = jnp.where(me > 0, 1.0, 0.0).astype(F32)
    has_next = jnp.where(me < n_ray - 1, 1.0, 0.0).astype(F32)
    has_below = jnp.where(t > 0, 1.0, 0.0).astype(F32)
    has_above = jnp.where(t < n_tile - 1, 1.0, 0.0).astype(F32)

    def transposed(half, first):
        pick[...] = dot(from_row, half).astype(BF16)
        sub = lax.broadcasted_iota(jnp.int32, (GROUP, depth), 0)
        upper = (sub & 3) < 2
        even = (sub & 1) == 0
        quad = lax.shift_right_logical(sub, 2)

        @pl.loop(0, groups // SPAN)
        def _(i):
            for h in range(SPAN):
                g = i * SPAN + h
                if first:
                    block_copy(g).wait()
                start = pl.multiple_of(g * GROUP, GROUP)
                lhs = pick[pl.ds(start, GROUP), :].astype(F32)
                lhs = jnp.concatenate(
                    [jnp.where(upper, lhs, 0.0), jnp.where(upper, 0.0, lhs)], axis=1
                ).astype(BF16)
                acc = jnp.zeros((GROUP, depth), F32)
                for q in range(GROUP // 4):
                    four = [held[start + 4 * q + k] for k in range(4)]
                    rhs = jnp.concatenate(
                        [
                            jnp.concatenate(four[:2], axis=1),
                            jnp.concatenate(four[2:], axis=1),
                        ],
                        axis=0,
                    )
                    both = dot(lhs, rhs)
                    one = jnp.where(even, both[:, :depth], both[:, depth:])
                    acc = jnp.where(quad == q, one, acc)
                prod[pl.ds(start, GROUP), :] = acc

        return dot(to_col, halves(prod[...], 0))

    def forward(field):
        picked = dot(from_col, halves(field, 1))
        lane = lax.broadcasted_iota(jnp.int32, (width, slots), 1)
        even = (lane & 1) == 0
        pair = lax.shift_right_logical(lane, 1)
        hi = picked[:, :depth].T
        lo = picked[:, depth:].T
        top = jnp.concatenate([jnp.where(even, hi, 0.0), jnp.where(even, lo, 0.0)], axis=1)
        bottom = jnp.concatenate([jnp.where(even, 0.0, hi), jnp.where(even, 0.0, lo)], axis=1)
        rhs = jnp.concatenate([top, bottom], axis=0).astype(BF16)

        def step(i, acc):
            for h in range(SPAN):
                start = (i * SPAN + h) * CHUNK
                lhs = jnp.concatenate(
                    [
                        jnp.concatenate([held[2 * (start + j)], held[2 * (start + j) + 1]], axis=1)
                        for j in range(CHUNK)
                    ],
                    axis=0,
                )
                out = dot(lhs, rhs)
                out = out[:, :slots] + out[:, slots:]
                for j in range(CHUNK):
                    acc = jnp.where(pair == start + j, out[j * width : (j + 1) * width], acc)
            return acc

        steps = slots // (2 * CHUNK * SPAN)
        acc = lax.fori_loop(0, steps, step, jnp.zeros((width, slots), F32))
        return dot(to_row, halves(acc.T, 0))

    def spread_z(s, z, squares):
        rows = parts_of(jnp.sum(squares, axis=0, keepdims=True))
        for p in range(n_ray):
            zbuf[s, p, 0:cells, :] = z[p * cells : (p + 1) * cells].astype(BF16)
            zbuf[s, p, cells : cells + TILE, :] = rows
        zrecv[s, me] = zbuf[s, me]
        return [
            send(
                zbuf.at[s, ray_peer(d)],
                zrecv.at[s, me],
                b_send.at[s, d - 1],
                b_recv.at[s, d - 1],
                (ray_peer(d), t),
            )
            for d in range(1, n_ray)
        ]

    def summed(ref, count):
        acc = ref[0].astype(F32)
        for i in range(1, count):
            acc = acc + ref[i].astype(F32)
        return acc

    own = pl.ds(pl.multiple_of(me * cells, cells), cells)
    before = pl.ds(pl.multiple_of(ray_peer(n_ray - 1) * cells, cells), cells)
    after = pl.ds(pl.multiple_of(ray_peer(1) * cells, cells), cells)

    def edges(ref, dst, sends, recvs):
        return [
            send(
                ref.at[pl.ds(cells - size_y, size_y)],
                dst.at[0],
                sends.at[0],
                recvs.at[0],
                (me, tile_peer(1)),
            ),
            send(
                ref.at[pl.ds(0, size_y)],
                dst.at[1],
                sends.at[1],
                recvs.at[1],
                (me, tile_peer(n_tile - 1)),
            ),
        ]

    arrived(copies)
    raw_rays = dfull[...]
    old_rays = None
    raw_cells = None
    v_prev = None
    for s in range(3):
        if s < 2:
            z = transposed(raw_rays.astype(BF16), s == 0)
            squares = fold(raw_rays)
            if s > 0:
                arrived(cell_copies)
                squares = squares + summed(small.at[1], n_tile)
            copies = spread_z(s, z, squares)
            if s > 0:
                arrived(q_copies)
                smooth = laplace(
                    qbuf[...],
                    qhalo_y[0] * has_prev,
                    qhalo_y[1] * has_next,
                    qhalo_x[0] * has_below,
                    qhalo_x[1] * has_above,
                    size_y,
                )
            arrived(copies)
            sums = summed(zrecv.at[s], n_ray)
            beta = jnp.sqrt(total(sums[cells:]) + EPS)
            if s == 0:
                v_raw = sums[:cells] / beta
            else:
                v_raw = (sums[:cells] + smooth) / beta - beta * v_prev
            field = vfull.at[s]
            field[own, :] = v_raw
            copies = to_rays(field.at[own], d_send.at[s], d_recv.at[s])
            halo_copies = edges(
                field.at[own], vhalo.at[s], h_send.at[s], h_recv.at[s]
            )
            arrived(copies)
            whole = field[...]
            small[2 * s, t] = fold(whole)
            alpha_copies = to_tiles(small.at[2 * s, t], s_send.at[2 * s], s_recv.at[2 * s])
            yrecv[s, t] = forward(whole).astype(BF16)
            y_copies = to_tiles(yrecv.at[s, t], e_send.at[s], e_recv.at[s])
            arrived(halo_copies)
            smooth_v = reg * laplace(
                v_raw,
                field[before, :] * has_prev,
                field[after, :] * has_next,
                vhalo[s, 0] * has_below,
                vhalo[s, 1] * has_above,
                size_y,
            )
            arrived(alpha_copies)
            alpha = jnp.sqrt(total(summed(small.at[2 * s], n_tile)) + EPS)
            v_now = v_raw / alpha
            if s == 0:
                new_cells = smooth_v / alpha
            else:
                new_cells = smooth_v / alpha - alpha * (raw_cells / beta)
            small[2 * s + 1, t] = fold(new_cells)
            cell_copies = to_tiles(
                small.at[2 * s + 1, t], s_send.at[2 * s + 1], s_recv.at[2 * s + 1]
            )
            if s == 0:
                qbuf[...] = reg * new_cells
                q_copies = edges(qbuf, qhalo_x, q_send, q_recv) + [
                    send(
                        qbuf, qhalo_y.at[0], q_send.at[2], q_recv.at[2], (ray_peer(1), t)
                    ),
                    send(
                        qbuf,
                        qhalo_y.at[1],
                        q_send.at[3],
                        q_recv.at[3],
                        (ray_peer(n_ray - 1), t),
                    ),
                ]
            old_rays = raw_rays / beta
            if s == 0:
                w_dir = v_now
                phibar = beta
                rhobar = alpha
                model = None
            else:
                rho = jnp.sqrt(rhobar * rhobar + beta * beta)
                cosine = rhobar / rho
                sine = beta / rho
                theta = sine * alpha
                rhobar = -cosine * alpha
                phi = cosine * phibar
                phibar = sine * phibar
                model = phi / rho * w_dir
                w_dir = v_now - theta / rho * w_dir
            arrived(y_copies)
            raw_rays = summed(yrecv.at[s], n_tile) / alpha - alpha * old_rays
            raw_cells = new_cells
            v_prev = v_now
        else:
            arrived(cell_copies)
            last[me] = fold(raw_rays) + summed(small.at[3], n_tile)
            earlier = list(started)
            copies = to_rays(last.at[me], f_send, f_recv)
            for copy in earlier:
                copy.wait_send()
            arrived(copies)
            beta = jnp.sqrt(total(summed(last, n_ray)) + EPS)
            ubuf[...] = raw_rays
            out_ref[...] = ubuf[mine, :] / beta
            rho = jnp.sqrt(rhobar * rhobar + beta * beta)
            phi = rhobar / rho * phibar
            model_ref[...] = model + phi / rho * w_dir
    for copy in copies:
        copy.wait_send()


def hand_out(model_in, rays_in, model_out, rays_out, sem):
    copies = [
        pltpu.make_async_copy(model_in, model_out, sem.at[0]),
        pltpu.make_async_copy(rays_in, rays_out, sem.at[1]),
    ]
    for copy in copies:
        copy.start()
    for copy in copies:
        copy.wait()


def shards(n_ray, n_tile, data, blocks, block_cols, block_rows, block_counts, reg_weight):
    size_x, size_y, depth = reg_weight.shape
    slots, width = blocks.shape[2:4]
    cells = size_x * size_y
    share = data.shape[0] // width
    row_blocks = share * n_tile
    dma = pltpu.SemaphoreType.DMA
    pairs = [
        dma((n_tile - 1,)),
        dma((n_tile - 1,)),
        dma((2, n_ray - 1)),
        dma((2, n_ray - 1)),
        dma((2, n_ray - 1)),
        dma((2, n_ray - 1)),
        dma((2, 2)),
        dma((2, 2)),
        dma((2, n_tile - 1)),
        dma((2, n_tile - 1)),
        dma((4, n_tile - 1)),
        dma((4, n_tile - 1)),
        dma((4,)),
        dma((4,)),
        dma((n_ray - 1,)),
        dma((n_ray - 1,)),
    ]
    vmem = pl.BlockSpec(memory_space=pltpu.VMEM)
    model, rays = pl.pallas_call(
        functools.partial(kernel, n_ray, n_tile, size_x, size_y),
        out_shape=(
            jax.ShapeDtypeStruct((cells, depth), F32),
            jax.ShapeDtypeStruct((share, width), F32),
        ),
        in_specs=[pl.BlockSpec(memory_space=pltpu.HBM)] * 6,
        out_specs=(vmem, vmem),
        scratch_shapes=[
            pltpu.VMEM((1, slots), jnp.int32),
            pltpu.VMEM((1, slots), jnp.int32),
            pltpu.VMEM((1, 1), jnp.int32),
            pltpu.VMEM((cells, depth), F32),
            pltpu.VMEM((slots, width, depth), BF16),
            pltpu.VMEM((slots, depth), BF16),
            pltpu.VMEM((slots, depth), F32),
            pltpu.VMEM((row_blocks, width), F32),
            pltpu.VMEM((2, n_ray, cells + TILE, depth), BF16),
            pltpu.VMEM((2, n_ray, cells + TILE, depth), BF16),
            pltpu.VMEM((2, n_ray * cells, depth), F32),
            pltpu.VMEM((2, 2, size_y, depth), F32),
            pltpu.VMEM((2, n_tile, row_blocks, width), BF16),
            pltpu.VMEM((4, n_tile, 8, depth), F32),
            pltpu.VMEM((cells, depth), F32),
            pltpu.VMEM((2, cells, depth), F32),
            pltpu.VMEM((2, size_y, depth), F32),
            pltpu.VMEM((n_ray, 8, depth), F32),
            pltpu.VMEM((row_blocks, width), F32),
            dma((5,)),
            dma((slots // GROUP,)),
        ]
        + pairs,
        compiler_params=pltpu.CompilerParams(
            collective_id=0, has_side_effects=True, vmem_limit_bytes=64 * 2**20
        ),
    )(
        data.reshape(share, width),
        blocks.reshape(slots, width, depth),
        block_cols.reshape(1, slots),
        block_rows.reshape(1, slots),
        block_counts,
        reg_weight.reshape(cells, depth),
    )
    hbm = pl.BlockSpec(memory_space=pltpu.HBM)
    model, rays = pl.pallas_call(
        hand_out,
        out_shape=(
            jax.ShapeDtypeStruct((cells, depth), F32),
            jax.ShapeDtypeStruct((share, width), F32),
        ),
        in_specs=[hbm, hbm],
        out_specs=(hbm, hbm),
        scratch_shapes=[dma((2,))],
        compiler_params=pltpu.CompilerParams(vmem_limit_bytes=64 * 2**20),
    )(model, rays)
    return model.reshape(size_x, size_y, depth), rays.reshape(-1)


def solution(mesh):
    return jax.shard_map(
        functools.partial(shards, mesh.shape["ray"], mesh.shape["tile"]),
        mesh=mesh,
        in_specs=(
            P(("ray", "tile")),
            P("ray", "tile", None, None, None),
            P("ray", "tile", None),
            P("ray", "tile", None),
            P("ray", "tile"),
            P("tile", "ray", None),
        ),
        out_specs=(P("tile", "ray", None), P(("ray", "tile"))),
        check_vma=False,
    )
```

```python
import functools

import jax
import jax.numpy as jnp
from jax import lax
from jax.experimental import pallas as pl
from jax.experimental.pallas import tpu as pltpu
from jax.sharding import PartitionSpec as P

MESH = pl.DeviceIdType.MESH
EPS = 1e-06
GROUP = 16
TILE = 16
SPAN = 8
CHUNK = 4
F32 = jnp.float32
BF16 = jnp.bfloat16


def total(x):
    return jnp.sum(jnp.sum(x, axis=0, keepdims=True), axis=1, keepdims=True)


def fold(x):
    acc = x[0:8] * x[0:8]
    for i in range(8, x.shape[0], 8):
        acc = acc + x[i : i + 8] * x[i : i + 8]
    return acc


def dot(a, b):
    return jnp.dot(a, b, preferred_element_type=F32)


def halves(x, axis):
    hi = x.astype(BF16)
    lo = (x - hi.astype(F32)).astype(BF16)
    return jnp.concatenate([hi, lo], axis=axis)


def parts_of(row):
    p1 = row.astype(BF16).astype(F32)
    p2 = (row - p1).astype(BF16).astype(F32)
    p3 = row - p1 - p2
    at = lax.broadcasted_iota(jnp.int32, (TILE, row.shape[1]), 0)
    tile = jnp.where(at == 0, p1, jnp.where(at == 1, p2, jnp.where(at == 2, p3, 0.0)))
    return tile.astype(BF16)


def laplace(cur, prev, nxt, xlo, xhi, size_y):
    rows, lanes = cur.shape
    iy = lax.broadcasted_iota(jnp.int32, cur.shape, 0) & (size_y - 1)
    iz = lax.broadcasted_iota(jnp.int32, cur.shape, 1)
    up = jnp.where(iy == 0, pltpu.roll(prev, rows - size_y + 1, 0), pltpu.roll(cur, 1, 0))
    down = jnp.where(
        iy == size_y - 1, pltpu.roll(nxt, size_y - 1, 0), pltpu.roll(cur, rows - 1, 0)
    )
    left = jnp.where(iz == 0, 0.0, pltpu.roll(cur, 1, 1))
    right = jnp.where(iz == lanes - 1, 0.0, pltpu.roll(cur, lanes - 1, 1))
    below = jnp.concatenate([xlo, cur[:-size_y]], axis=0)
    above = jnp.concatenate([cur[size_y:], xhi], axis=0)
    return 6.0 * cur - (above + below + down + up + right + left)


def kernel(
    n_ray,
    n_tile,
    size_x,
    size_y,
    data_hbm,
    blocks_ref,
    cols_hbm,
    rows_hbm,
    count_hbm,
    reg_hbm,
    model_ref,
    out_ref,
    cols_ref,
    rows_ref,
    count_ref,
    reg_ref,
    held,
    pick,
    prod,
    dfull,
    zbuf,
    zrecv,
    vfull,
    vhalo,
    yrecv,
    small,
    qbuf,
    qhalo_y,
    qhalo_x,
    last,
    ubuf,
    in_sem,
    block_sem,
    a_send,
    a_recv,
    b_send,
    b_recv,
    d_send,
    d_recv,
    h_send,
    h_recv,
    e_send,
    e_recv,
    s_send,
    s_recv,
    q_send,
    q_recv,
    f_send,
    f_recv,
):
    me = lax.axis_index("ray")
    t = lax.axis_index("tile")
    slots, width, depth = held.shape
    cells = size_x * size_y
    tile_cols = n_ray * cells
    grid_y = n_ray * size_y
    share = data_hbm.shape[0]
    row_blocks = share * n_tile
    groups = slots // GROUP

    def block_copy(g):
        part = pl.ds(g * GROUP, GROUP)
        return pltpu.make_async_copy(blocks_ref.at[part], held.at[part], block_sem.at[g])

    mine = pl.ds(pl.multiple_of(t * share, share), share)
    inputs = [
        pltpu.make_async_copy(src, dst, in_sem.at[i])
        for i, (src, dst) in enumerate(
            [
                (data_hbm, dfull.at[mine]),
                (cols_hbm, cols_ref),
                (rows_hbm, rows_ref),
                (count_hbm, count_ref),
                (reg_hbm, reg_ref),
            ]
        )
    ]
    for copy in inputs:
        copy.start()
    for g in range(groups):
        block_copy(g).start()

    def ray_peer(d):
        return lax.rem(me + d, n_ray)

    def tile_peer(d):
        return lax.rem(t + d, n_tile)

    bar = pltpu.get_barrier_semaphore()
    for d in range(1, n_ray):
        pl.semaphore_signal(bar, inc=1, device_id=(ray_peer(d), t), device_id_type=MESH)
    for d in range(1, n_tile):
        pl.semaphore_signal(bar, inc=1, device_id=(me, tile_peer(d)), device_id_type=MESH)
    pl.semaphore_wait(bar, n_ray + n_tile - 2)

    started = []

    def send(src, dst, send_sem, recv_sem, device):
        copy = pltpu.make_async_remote_copy(
            src_ref=src,
            dst_ref=dst,
            send_sem=send_sem,
            recv_sem=recv_sem,
            device_id=device,
            device_id_type=MESH,
        )
        copy.start()
        started.append(copy)
        return copy

    def to_tiles(ref, sends, recvs):
        return [
            send(ref, ref, sends.at[d - 1], recvs.at[d - 1], (me, tile_peer(d)))
            for d in range(1, n_tile)
        ]

    def to_rays(ref, sends, recvs):
        return [
            send(ref, ref, sends.at[d - 1], recvs.at[d - 1], (ray_peer(d), t))
            for d in range(1, n_ray)
        ]

    def arrived(copies):
        for copy in copies:
            copy.wait_recv()

    inputs[0].wait()
    copies = to_tiles(dfull.at[mine], a_send, a_recv)

    for copy in inputs[1:]:
        copy.wait()
    live = lax.broadcasted_iota(jnp.int32, (1, slots), 1) < count_ref[...]
    col = cols_ref[...]
    col_x = lax.shift_right_logical(col, grid_y.bit_length() - 1)
    col_y = col & (grid_y - 1)
    place = (
        lax.shift_right_logical(col_y, size_y.bit_length() - 1) * cells
        + col_x * size_y
        + (col_y & (size_y - 1))
    )
    place = jnp.where(live, place, -1)
    row = jnp.where(live, rows_ref[...], -1)
    to_col = jnp.where(
        lax.broadcasted_iota(jnp.int32, (tile_cols, slots), 0) == place, 1.0, 0.0
    ).astype(F32)
    to_row = jnp.where(
        lax.broadcasted_iota(jnp.int32, (row_blocks, slots), 0) == row, 1.0, 0.0
    ).astype(F32)
    from_col = to_col.T.astype(BF16)
    from_row = to_row.T.astype(BF16)
    to_col = jnp.concatenate([to_col, to_col], axis=1).astype(BF16)
    to_row = jnp.concatenate([to_row, to_row], axis=1).astype(BF16)
    reg = reg_ref[...]
    has_prev = jnp.where(me > 0, 1.0, 0.0).astype(F32)
    has_next = jnp.where(me < n_ray - 1, 1.0, 0.0).astype(F32)
    has_below = jnp.where(t > 0, 1.0, 0.0).astype(F32)
    has_above = jnp.where(t < n_tile - 1, 1.0, 0.0).astype(F32)

    def transposed(half, first):
        pick[...] = dot(from_row, half).astype(BF16)
        sub = lax.broadcasted_iota(jnp.int32, (GROUP, depth), 0)
        upper = (sub & 3) < 2
        even = (sub & 1) == 0
        quad = lax.shift_right_logical(sub, 2)

        @pl.loop(0, groups // SPAN)
        def _(i):
            for h in range(SPAN):
                g = i * SPAN + h
                if first:
                    block_copy(g).wait()
                start = pl.multiple_of(g * GROUP, GROUP)
                lhs = pick[pl.ds(start, GROUP), :].astype(F32)
                lhs = jnp.concatenate(
                    [jnp.where(upper, lhs, 0.0), jnp.where(upper, 0.0, lhs)], axis=1
                ).astype(BF16)
                acc = jnp.zeros((GROUP, depth), F32)
                for q in range(GROUP // 4):
                    four = [held[start + 4 * q + k] for k in range(4)]
                    rhs = jnp.concatenate(
                        [
                            jnp.concatenate(four[:2], axis=1),
                            jnp.concatenate(four[2:], axis=1),
                        ],
                        axis=0,
                    )
                    both = dot(lhs, rhs)
                    one = jnp.where(even, both[:, :depth], both[:, depth:])
                    acc = jnp.where(quad == q, one, acc)
                prod[pl.ds(start, GROUP), :] = acc

        return dot(to_col, halves(prod[...], 0))

    def forward(field):
        picked = dot(from_col, halves(field, 1))
        lane = lax.broadcasted_iota(jnp.int32, (width, slots), 1)
        even = (lane & 1) == 0
        pair = lax.shift_right_logical(lane, 1)
        hi = picked[:, :depth].T
        lo = picked[:, depth:].T
        top = jnp.concatenate([jnp.where(even, hi, 0.0), jnp.where(even, lo, 0.0)], axis=1)
        bottom = jnp.concatenate([jnp.where(even, 0.0, hi), jnp.where(even, 0.0, lo)], axis=1)
        rhs = jnp.concatenate([top, bottom], axis=0).astype(BF16)

        def step(i, acc):
            for h in range(SPAN):
                start = (i * SPAN + h) * CHUNK
                lhs = jnp.concatenate(
                    [
                        jnp.concatenate([held[2 * (start + j)], held[2 * (start + j) + 1]], axis=1)
                        for j in range(CHUNK)
                    ],
                    axis=0,
                )
                out = dot(lhs, rhs)
                out = out[:, :slots] + out[:, slots:]
                for j in range(CHUNK):
                    acc = jnp.where(pair == start + j, out[j * width : (j + 1) * width], acc)
            return acc

        steps = slots // (2 * CHUNK * SPAN)
        acc = lax.fori_loop(0, steps, step, jnp.zeros((width, slots), F32))
        return dot(to_row, halves(acc.T, 0))

    def spread_z(s, z, squares):
        rows = parts_of(jnp.sum(squares, axis=0, keepdims=True))
        for p in range(n_ray):
            zbuf[s, p, 0:cells, :] = z[p * cells : (p + 1) * cells].astype(BF16)
            zbuf[s, p, cells : cells + TILE, :] = rows
        zrecv[s, me] = zbuf[s, me]
        return [
            send(
                zbuf.at[s, ray_peer(d)],
                zrecv.at[s, me],
                b_send.at[s, d - 1],
                b_recv.at[s, d - 1],
                (ray_peer(d), t),
            )
            for d in range(1, n_ray)
        ]

    def summed(ref, count):
        acc = ref[0].astype(F32)
        for i in range(1, count):
            acc = acc + ref[i].astype(F32)
        return acc

    own = pl.ds(pl.multiple_of(me * cells, cells), cells)
    before = pl.ds(pl.multiple_of(ray_peer(n_ray - 1) * cells, cells), cells)
    after = pl.ds(pl.multiple_of(ray_peer(1) * cells, cells), cells)

    def edges(ref, dst, sends, recvs):
        return [
            send(
                ref.at[pl.ds(cells - size_y, size_y)],
                dst.at[0],
                sends.at[0],
                recvs.at[0],
                (me, tile_peer(1)),
            ),
            send(
                ref.at[pl.ds(0, size_y)],
                dst.at[1],
                sends.at[1],
                recvs.at[1],
                (me, tile_peer(n_tile - 1)),
            ),
        ]

    arrived(copies)
    raw_rays = dfull[...]
    old_rays = None
    raw_cells = None
    v_prev = None
    for s in range(3):
        if s < 2:
            z = transposed(raw_rays.astype(BF16), s == 0)
            squares = fold(raw_rays)
            if s > 0:
                arrived(cell_copies)
                squares = squares + summed(small.at[1], n_tile)
            copies = spread_z(s, z, squares)
            if s > 0:
                arrived(q_copies)
                smooth = laplace(
                    qbuf[...],
                    qhalo_y[0] * has_prev,
                    qhalo_y[1] * has_next,
                    qhalo_x[0] * has_below,
                    qhalo_x[1] * has_above,
                    size_y,
                )
            arrived(copies)
            sums = summed(zrecv.at[s], n_ray)
            beta = jnp.sqrt(total(sums[cells:]) + EPS)
            if s == 0:
                v_raw = sums[:cells] / beta
            else:
                v_raw = (sums[:cells] + smooth) / beta - beta * v_prev
            field = vfull.at[s]
            field[own, :] = v_raw
            copies = to_rays(field.at[own], d_send.at[s], d_recv.at[s])
            halo_copies = edges(
                field.at[own], vhalo.at[s], h_send.at[s], h_recv.at[s]
            )
            arrived(copies)
            whole = field[...]
            small[2 * s, t] = fold(whole)
            alpha_copies = to_tiles(small.at[2 * s, t], s_send.at[2 * s], s_recv.at[2 * s])
            yrecv[s, t] = forward(whole).astype(BF16)
            y_copies = to_tiles(yrecv.at[s, t], e_send.at[s], e_recv.at[s])
            arrived(halo_copies)
            smooth_v = reg * laplace(
                v_raw,
                field[before, :] * has_prev,
                field[after, :] * has_next,
                vhalo[s, 0] * has_below,
                vhalo[s, 1] * has_above,
                size_y,
            )
            arrived(alpha_copies)
            alpha = jnp.sqrt(total(summed(small.at[2 * s], n_tile)) + EPS)
            v_now = v_raw / alpha
            if s == 0:
                new_cells = smooth_v / alpha
            else:
                new_cells = smooth_v / alpha - alpha * (raw_cells / beta)
            small[2 * s + 1, t] = fold(new_cells)
            cell_copies = to_tiles(
                small.at[2 * s + 1, t], s_send.at[2 * s + 1], s_recv.at[2 * s + 1]
            )
            if s == 0:
                qbuf[...] = reg * new_cells
                q_copies = edges(qbuf, qhalo_x, q_send, q_recv) + [
                    send(
                        qbuf, qhalo_y.at[0], q_send.at[2], q_recv.at[2], (ray_peer(1), t)
                    ),
                    send(
                        qbuf,
                        qhalo_y.at[1],
                        q_send.at[3],
                        q_recv.at[3],
                        (ray_peer(n_ray - 1), t),
                    ),
                ]
            old_rays = raw_rays / beta
            if s == 0:
                w_dir = v_now
                phibar = beta
                rhobar = alpha
                model = None
            else:
                rho = jnp.sqrt(rhobar * rhobar + beta * beta)
                cosine = rhobar / rho
                sine = beta / rho
                theta = sine * alpha
                rhobar = -cosine * alpha
                phi = cosine * phibar
                phibar = sine * phibar
                model = phi / rho * w_dir
                w_dir = v_now - theta / rho * w_dir
            arrived(y_copies)
            raw_rays = summed(yrecv.at[s], n_tile) / alpha - alpha * old_rays
            raw_cells = new_cells
            v_prev = v_now
        else:
            arrived(cell_copies)
            last[me] = fold(raw_rays) + summed(small.at[3], n_tile)
            earlier = list(started)
            copies = to_rays(last.at[me], f_send, f_recv)
            for copy in earlier:
                copy.wait_send()
            arrived(copies)
            beta = jnp.sqrt(total(summed(last, n_ray)) + EPS)
            ubuf[...] = raw_rays
            out_ref[...] = ubuf[mine, :] / beta
            rho = jnp.sqrt(rhobar * rhobar + beta * beta)
            phi = rhobar / rho * phibar
            model_ref[...] = model + phi / rho * w_dir
    for copy in copies:
        copy.wait_send()


def hand_out(model_in, rays_in, model_out, rays_out, sem):
    copies = [
        pltpu.make_async_copy(model_in, model_out, sem.at[0]),
        pltpu.make_async_copy(rays_in, rays_out, sem.at[1]),
    ]
    for copy in copies:
        copy.start()
    for copy in copies:
        copy.wait()


def shards(n_ray, n_tile, data, blocks, block_cols, block_rows, block_counts, reg_weight):
    size_x, size_y, depth = reg_weight.shape
    slots, width = blocks.shape[2:4]
    cells = size_x * size_y
    share = data.shape[0] // width
    row_blocks = share * n_tile
    dma = pltpu.SemaphoreType.DMA
    pairs = [
        dma((n_tile - 1,)),
        dma((n_tile - 1,)),
        dma((2, n_ray - 1)),
        dma((2, n_ray - 1)),
        dma((2, n_ray - 1)),
        dma((2, n_ray - 1)),
        dma((2, 2)),
        dma((2, 2)),
        dma((2, n_tile - 1)),
        dma((2, n_tile - 1)),
        dma((4, n_tile - 1)),
        dma((4, n_tile - 1)),
        dma((4,)),
        dma((4,)),
        dma((n_ray - 1,)),
        dma((n_ray - 1,)),
    ]
    vmem = pl.BlockSpec(memory_space=pltpu.VMEM)
    model, rays = pl.pallas_call(
        functools.partial(kernel, n_ray, n_tile, size_x, size_y),
        out_shape=(
            jax.ShapeDtypeStruct((cells, depth), F32),
            jax.ShapeDtypeStruct((share, width), F32),
        ),
        in_specs=[pl.BlockSpec(memory_space=pltpu.HBM)] * 6,
        out_specs=(vmem, vmem),
        scratch_shapes=[
            pltpu.VMEM((1, slots), jnp.int32),
            pltpu.VMEM((1, slots), jnp.int32),
            pltpu.VMEM((1, 1), jnp.int32),
            pltpu.VMEM((cells, depth), F32),
            pltpu.VMEM((slots, width, depth), BF16),
            pltpu.VMEM((slots, depth), BF16),
            pltpu.VMEM((slots, depth), F32),
            pltpu.VMEM((row_blocks, width), F32),
            pltpu.VMEM((2, n_ray, cells + TILE, depth), BF16),
            pltpu.VMEM((2, n_ray, cells + TILE, depth), BF16),
            pltpu.VMEM((2, n_ray * cells, depth), F32),
            pltpu.VMEM((2, 2, size_y, depth), F32),
            pltpu.VMEM((2, n_tile, row_blocks, width), BF16),
            pltpu.VMEM((4, n_tile, 8, depth), F32),
            pltpu.VMEM((cells, depth), F32),
            pltpu.VMEM((2, cells, depth), F32),
            pltpu.VMEM((2, size_y, depth), F32),
            pltpu.VMEM((n_ray, 8, depth), F32),
            pltpu.VMEM((row_blocks, width), F32),
            dma((5,)),
            dma((slots // GROUP,)),
        ]
        + pairs,
        compiler_params=pltpu.CompilerParams(
            collective_id=0, has_side_effects=True, vmem_limit_bytes=64 * 2**20
        ),
    )(
        data.reshape(share, width),
        blocks.reshape(slots, width, depth),
        block_cols.reshape(1, slots),
        block_rows.reshape(1, slots),
        block_counts,
        reg_weight.reshape(cells, depth),
    )
    hbm = pl.BlockSpec(memory_space=pltpu.HBM)
    model, rays = pl.pallas_call(
        hand_out,
        out_shape=(
            jax.ShapeDtypeStruct((cells, depth), F32),
            jax.ShapeDtypeStruct((share, width), F32),
        ),
        in_specs=[hbm, hbm],
        out_specs=(hbm, hbm),
        scratch_shapes=[dma((2,))],
        compiler_params=pltpu.CompilerParams(vmem_limit_bytes=64 * 2**20),
    )(model, rays)
    return model.reshape(size_x, size_y, depth), rays.reshape(-1)


def solution(mesh):
    return jax.shard_map(
        functools.partial(shards, mesh.shape["ray"], mesh.shape["tile"]),
        mesh=mesh,
        in_specs=(
            P(("ray", "tile")),
            P("ray", "tile", None, None, None),
            P("ray", "tile", None),
            P("ray", "tile", None),
            P("ray", "tile"),
            P("tile", "ray", None),
        ),
        out_specs=(P("tile", "ray", None), P(("ray", "tile"))),
        check_vma=False,
    )
```
